512 devices in a mesh: tm: 64 (over y_hi, z, x), space: 8 (over y_lo, core).
Axes of the slice: x: 4, y: 8 (y_hi: 2, y_lo: 4; y = y_hi * 4 + y_lo), z: 8, core: 2. Of those that a mesh axis runs over, the one named last changes fastest.
Arguments:
- guess: float32 [256, 12, 48, 512], P('tm', None, 'space'), may hold values from -6 to 6
- forcing: float32 [12, 48, 512], P(None, 'space'), may hold values from -6 to 6
- coarse_gain: float32 [12, 48, 512], P(None, 'space'), may hold values from 0.9 to 1
- kernel_levels: float32 [8], replicated, may hold values from 0.002 to 0.03
- kernel_code: int32 [12, 12], replicated, may hold values from 0 to 7
- settle_levels: float32 [4], replicated, may hold values from 0.02 to 0.15
- settle_class: int32 [12], replicated, may hold values from 0 to 3
Outputs:
- updated: float32 [256, 12, 48, 512], P('tm', None, 'space')
- correction: float32 [64, 12, 48, 512], P('tm', None, 'space')
The draws below stay inside these ranges and needn't reach their ends.
All inputs are finite; a program needn't handle non-finite values.
Results may differ from the reference program's by a relative error of at most 0.0001.
Values sent between devices are 32-bit elements; how exact they have to be, the bound alone decides.
No kernel may reach another device: no remote copies, remote signals or barrier semaphores. Data moves between devices by JAX's collectives and lax.ppermute only.
A program may use at most 64 MiB of HBM per device.

```python
import math
import jax
import jax.numpy as jnp
from jax import lax

C = 12
TPD = 4
NY = 16
NZ = 32
KL = 8
SL = 4
NX = 48
YZ = 512
NT = 256
N_TM = 64


def place_ends(values, rng, smallest, high):
    longest = values.shape.index(max(values.shape))
    spots = []
    for shift in (0, 1):
        where = [jax.random.randint(jax.random.fold_in(rng, axis), (), 0, length) for axis, length in enumerate(values.shape)]
        where[longest] = (where[longest] + shift) % values.shape[longest]
        spots.append(tuple(where))
    return values.at[spots[0]].set(smallest).at[spots[1]].set(high)


def shard_levels(key, dims, shards, least, top_value):
    gain = 1.0
    for axis_at, shards_of in shards:
        draws = jax.random.uniform(jax.random.fold_in(jax.random.fold_in(key, 6), axis_at), (shards_of,), jnp.float32, least / len(shards), top_value / len(shards))
        gain = gain * jnp.repeat(jnp.exp(draws), dims[axis_at] // shards_of).reshape((-1,) + (1,) * (len(dims) - 1 - axis_at))
    return gain


def noise(stream_key, dims, scale, limit, shards=(), held_as=jnp.bfloat16):
    array = scale * jax.random.normal(stream_key, dims, jnp.float32)
    if shards:
        array = array * shard_levels(stream_key, dims, shards, -0.22, 0.18)
    return jnp.clip(array, -limit, limit).astype(held_as)


def setup_inputs(seed: int = 0) -> dict:
    seeds = jax.random.split(jax.random.key(seed), 8)
    guess = noise(seeds[0], (NT, C, NX, YZ), 1.0, 6.0, ((0, 64), (2, 8)), jnp.float32)
    forcing = noise(seeds[1], (C, NX, YZ), 1.0, 6.0, ((1, 8),), jnp.float32)
    coarse_gain = jnp.clip(0.9 + 0.100000024 * jax.random.uniform(seeds[2], (C, NX, YZ), jnp.float32) ** shard_levels(seeds[2], (C, NX, YZ), ((1, 8),), -0.2, 0.2), 0.9, 1.0)
    kernel_levels = jnp.clip(jnp.exp(jax.random.uniform(seeds[3], (KL,), jnp.float32, math.log(0.002), math.log(0.03))), 0.002, 0.03)
    kernel_code = place_ends(jax.random.randint(seeds[4], (C, C), 0, KL), jax.random.fold_in(seeds[4], 1), 0, KL - 1).astype(jnp.int32)
    settle_levels = jnp.clip(jax.random.uniform(seeds[5], (SL,), jnp.float32, 0.02, 0.15), 0.02, 0.15)
    settle_class = place_ends(jax.random.randint(seeds[6], (C,), 0, SL), jax.random.fold_in(seeds[6], 1), 0, SL - 1).astype(jnp.int32)
    return dict(guess=guess, forcing=forcing, coarse_gain=coarse_gain, kernel_levels=kernel_levels, kernel_code=kernel_code, settle_levels=settle_levels, settle_class=settle_class)


def operators(kernel_levels, kernel_code, settle_levels, settle_class):
    level_ids = jnp.arange(KL, dtype=jnp.int32)
    kernel = jnp.sum(jnp.where(kernel_code[:, :, None] == level_ids, kernel_levels, 0.0), axis=-1)
    kmat = kernel - jnp.diag(jnp.sum(kernel, axis=0))
    speed_ids = jnp.arange(SL, dtype=jnp.int32)
    speed = jnp.sum(jnp.where(settle_class[:, None] == speed_ids, settle_levels, 0.0), axis=-1)
    return kmat, speed


def fine_step(state, forcing, kmat, speed):
    width = state.shape[-1]
    place = jnp.arange(width, dtype=jnp.int32)
    zpos = place % NZ
    ypos = place // NZ
    pad_cfg = [(0, 0)] * (state.ndim - 2) + [(1, 1), (0, 0)]
    padded = jnp.pad(state, pad_cfg)
    xsum = padded[..., 2:, :] + padded[..., :-2, :]
    upper = jnp.where(zpos < NZ - 1, jnp.roll(state, -1, axis=-1), 0.0)
    lower = jnp.where(zpos > 0, jnp.roll(state, 1, axis=-1), 0.0)
    ahead = jnp.where(ypos < NY - 1, jnp.roll(state, -NZ, axis=-1), 0.0)
    behind = jnp.where(ypos > 0, jnp.roll(state, NZ, axis=-1), 0.0)
    laplace = xsum + upper + lower + ahead + behind - 6.0 * state
    mixing = jnp.einsum("ij,...jxs->...ixs", kmat, state, precision=lax.Precision.HIGHEST)
    return state + 0.08 * laplace + speed[:, None, None] * (upper - state) + mixing + 0.1 * forcing


def reference(guess, forcing, coarse_gain, kernel_levels, kernel_code, settle_levels, settle_class):
    kmat, speed = operators(kernel_levels, kernel_code, settle_levels, settle_class)
    states = guess.reshape(N_TM, TPD, C, guess.shape[2], guess.shape[3])

    def relax(states):
        for j in range(1, TPD):
            states = states.at[:, j].set(fine_step(states[:, j - 1], forcing, kmat, speed))
        return states

    states = relax(states)
    states = states.at[1:, 0].set(fine_step(states[:-1, TPD - 1], forcing, kmat, speed))
    states = relax(states)
    tail = fine_step(states[:-1, TPD - 1], forcing, kmat, speed) - states[1:, 0]
    resid = jnp.concatenate([jnp.zeros_like(tail[:1]), tail], axis=0)

    def advance(carry, item):
        value = coarse_gain * carry + item
        return value, value

    start = jnp.zeros_like(resid[0])
    last, rest = lax.scan(advance, start, resid[1:])
    correction = jnp.concatenate([start[None], rest], axis=0)
    states = states.at[:, 0].add(correction)
    states = relax(states)
    return states.reshape(guess.shape), correction
```

```python
import functools

import jax
import jax.numpy as jnp
from jax import lax
from jax.experimental import pallas as pl
from jax.experimental.pallas import tpu as pltpu
from jax.sharding import PartitionSpec as P

F32 = jnp.float32
C = 12
NY = 16
NZ = 32
PLANES = 6
NX = 48
SLICES = 4
ROWS = 4
OWN = PLANES * ROWS
HALO = 4 * ROWS
WIN = 64
BASE = 5 * ROWS
PIECE = 5
VMEM = pl.BlockSpec(memory_space=pltpu.VMEM)
SMEM = pl.BlockSpec(memory_space=pltpu.SMEM)
PARAMS = pltpu.CompilerParams(vmem_limit_bytes=32 * 1024 * 1024)


def arr(*shape):
    return jax.ShapeDtypeStruct(shape, F32)


def even_place():
    return lax.axis_index("space") % 2 == 0


def put_sends(first, last, near, far):
    even = even_place()

    @pl.when(even)
    def _():
        near[...] = last()
        far[...] = first()

    @pl.when(jnp.logical_not(even))
    def _():
        near[...] = first()
        far[...] = last()


def put_halo(buf, near, far):
    even = even_place()

    @pl.when(even)
    def _():
        buf[:, 4:BASE, :] = far()
        buf[:, BASE + OWN : 60, :] = near()

    @pl.when(jnp.logical_not(even))
    def _():
        buf[:, 4:BASE, :] = near()
        buf[:, BASE + OWN : 60, :] = far()


def prep_kernel(guess, forcing, gain, levels, code, settle, klass, own, near, far, gain_out, kmat, speed):
    for j in range(C):
        total = None
        col = []
        for i in range(C):
            v = levels[code[i, j]]
            col.append(v)
            total = v if total is None else total + v
        for i in range(C):
            if i == j:
                w = settle[klass[i]]
                speed[i] = w
                kmat[i, j] = (col[i] - total) + (1.0 - 0.48) - w
            else:
                kmat[i, j] = col[i]
    for c in range(C):
        own[c] = guess[pl.ds(c * OWN * SLICES, OWN, stride=SLICES), :]
        for r in range(ROWS):
            lanes = pl.ds(128 * r, 128)
            own[C + c, pl.ds(r, PLANES, stride=ROWS), :] = forcing[c, :, lanes] * 0.1
            gain_out[pl.ds(c * OWN + r, PLANES, stride=ROWS), :] = gain[c, :, lanes]
    gain_out[C * OWN :, :] = jnp.zeros((64 * PIECE - C * OWN, 128), F32)
    put_sends(lambda: own[:, :HALO, :], lambda: own[:, OWN - HALO :, :], near, far)


def coefficients(kmat, speed, kv, wup, wfix, mask):
    lane = lax.broadcasted_iota(jnp.int32, (8, 128), 1)
    row = lax.broadcasted_iota(jnp.int32, (8, 128), 0)
    z = lane % NZ
    edge_row = row % ROWS
    for i in range(C):
        for j in range(C):
            kv[i * C + j] = jnp.full((8, 128), kmat[i, j], F32)
        wup[i] = jnp.where(z < NZ - 1, 0.08 + speed[i], 0.0)
    wfix[0] = jnp.where(z > 0, F32(0.08), F32(0.0))
    wfix[1] = jnp.where(jnp.logical_and(lane >= 96, edge_row == ROWS - 1), F32(0.0), F32(0.08))
    wfix[2] = jnp.where(jnp.logical_and(lane < 32, edge_row == 0), F32(0.0), F32(0.08))
    start = lax.axis_index("space") * PLANES - 5
    for t in range(WIN // 8):
        plane = start + 2 * t + row // ROWS
        inside = jnp.logical_and(plane >= 0, plane < NX)
        mask[t] = jnp.where(inside, F32(1.0), F32(0.0))


def clear_edges(buf):
    z = jnp.zeros((C, 8, 128), F32)
    buf[:, 0:8, :] = z
    buf[:, WIN - 8 : WIN, :] = z


def block_step(src, dst, fwin, t, kv, wup, wfix, mask):
    lane = lax.broadcasted_iota(jnp.int32, (8, 128), 1)
    row = lax.broadcasted_iota(jnp.int32, (8, 128), 0)
    low = row < ROWS
    right = lane >= 96
    left = lane < 32
    wdn, wah, wbe = wfix[0], wfix[1], wfix[2]

    def rows(k):
        return pl.ds(pl.multiple_of((t + k) * 8, 8), 8)

    acc = []
    for i in range(C):
        p = [src[i, rows(k), :] for k in (-1, 0, 1, 2)]
        q = [pltpu.roll(v, 4, 0) for v in p]
        pair = []
        for k in (0, 1):
            c = p[k + 1]
            xs = q[k + 1] + jnp.where(low, q[k], q[k + 2])
            up = pltpu.roll(c, 127, 1)
            dn = pltpu.roll(c, 1, 1)
            ra = pltpu.roll(c, 96, 1)
            rb = pltpu.roll(c, 32, 1)
            ah = jnp.where(right, pltpu.roll(ra, 7, 0), ra)
            be = jnp.where(left, pltpu.roll(rb, 1, 0), rb)
            new = fwin[i, rows(k), :] + 0.08 * xs
            new = new + wup[i] * up
            new = new + wdn * dn
            new = new + wah * ah
            new = new + wbe * be
            pair.append(new)
        acc.append(pair)
    for j in range(C):
        c = [src[j, rows(k), :] for k in (0, 1)]
        for i in range(C):
            w = kv[i * C + j]
            acc[i] = [acc[i][k] + w * c[k] for k in (0, 1)]
    for k in (0, 1):
        m = mask[t + k]
        for i in range(C):
            dst[i, rows(k), :] = acc[i][k] * m


def steps(bufs, fwin, plan, coefs):
    for s, (first, count) in enumerate(plan):
        src, dst = bufs[s % 2], bufs[(s + 1) % 2]

        @pl.loop(0, count)
        def _(b):
            block_step(src, dst, fwin, first + 2 * b, *coefs)


FOUR = ((1, 3), (1, 3), (2, 2), (2, 2))


def first_kernel(own, near, far, kmat, speed, state, send_near, send_far, fwin, a, b, kv, wup, wfix, mask):
    coefs = (kv, wup, wfix, mask)
    coefficients(kmat, speed, *coefs)
    clear_edges(a)
    clear_edges(b)
    clear_edges(fwin)
    a[:, BASE : BASE + OWN, :] = own[:C]
    fwin[:, BASE : BASE + OWN, :] = own[C:]
    put_halo(a, lambda: near[:C], lambda: far[:C])
    put_halo(fwin, lambda: near[C:], lambda: far[C:])
    steps((a, b), fwin, FOUR, coefs)
    state[...] = a[:, BASE : BASE + OWN, :]
    put_sends(lambda: state[:, :HALO, :], lambda: state[:, OWN - HALO :, :], send_near, send_far)


def second_kernel(state, near, far, fwin, gain, kmat, speed, out, a, b, kv, wup, wfix, mask):
    coefs = (kv, wup, wfix, mask)
    coefficients(kmat, speed, *coefs)
    clear_edges(a)
    clear_edges(b)
    a[:, BASE : BASE + OWN, :] = state[...]
    put_halo(a, lambda: near[...], lambda: far[...])
    steps((a, b), fwin, FOUR, coefs)
    use = jnp.where(lax.axis_index("tm") > 0, F32(1.0), F32(0.0))
    for c in range(C):
        here = pl.ds(c * OWN, OWN)
        out[here, :] = a[c, BASE : BASE + OWN, :] - use * (gain[here, :] * state[c])
    out[C * OWN :, :] = jnp.zeros((64 * PIECE - C * OWN, 128), F32)


def scan_kernel(pieces, gain, out):
    count = pieces.shape[0] // PIECE
    mine = gain[0]
    running = pieces[0:PIECE, :]
    out[0 : 2 * PIECE, :] = jnp.zeros((2 * PIECE, 128), F32)
    for k in range(2, count):
        out[k * PIECE : (k + 1) * PIECE, :] = running
        if k + 1 < count:
            m = k - 1
            running = mine * running + pieces[m * PIECE : (m + 1) * PIECE, :]


def gather_kernel(pieces, shifted, own, state, near, far, corr):
    k = lax.axis_index("tm")

    @pl.when(k == 0)
    def _():
        state[...] = own[:C]

    @pl.when(k == 1)
    def _():
        state[...] = shifted[...]

    @pl.when(k >= 2)
    def _():
        for c in range(C):
            state[c] = pieces[c * OWN : (c + 1) * OWN, :]

    put_sends(lambda: state[:, :HALO, :], lambda: state[:, OWN - HALO :, :], near, far)

    @pl.when(k < 2)
    def _():
        corr[...] = jnp.zeros_like(corr)

    @pl.when(k >= 2)
    def _():
        for c in range(C):
            corr[c * OWN : (c + 1) * OWN, :] = state[c] - shifted[c]


def last_kernel(state, near, far, fwin, kmat, speed, out, a, b, kv, wup, wfix, mask):
    coefs = (kv, wup, wfix, mask)
    coefficients(kmat, speed, *coefs)
    clear_edges(a)
    clear_edges(b)
    a[:, BASE : BASE + OWN, :] = state[...]
    put_halo(a, lambda: near[...], lambda: far[...])

    def emit(buf, j):
        for c in range(C):
            out[pl.ds(c * OWN * SLICES + j, OWN, stride=SLICES), :] = buf[c, BASE : BASE + OWN, :]

    emit(a, 0)
    bufs = (a, b)
    for j, one in enumerate(((1, 3), (2, 2), (2, 2))):
        src, dst = bufs[j % 2], bufs[(j + 1) % 2]
        steps((src, dst), fwin, (one,), coefs)
        emit(dst, j + 1)


WORK = [
    pltpu.VMEM((C, WIN, 128), F32),
    pltpu.VMEM((C, WIN, 128), F32),
    pltpu.VMEM((C * C, 8, 128), F32),
    pltpu.VMEM((C, 8, 128), F32),
    pltpu.VMEM((3, 8, 128), F32),
    pltpu.VMEM((WIN // 8, 8, 128), F32),
]


def call(kernel, ins, outs, out_specs=None, scratch=()):
    specs = out_specs or [VMEM] * len(outs)
    in_specs = [spec for _, spec in ins]
    return pl.pallas_call(
        kernel,
        out_shape=outs,
        in_specs=in_specs,
        out_specs=specs,
        scratch_shapes=list(scratch),
        compiler_params=PARAMS,
        name=kernel.__name__,
    )(*[value for value, _ in ins])


def exchange(near, far):
    places = lax.axis_size("space")
    inner = [(i, i ^ 1) for i in range(places)]
    outer = [(i, j) for i in range(places) for j in [i - 1 if i % 2 == 0 else i + 1] if 0 <= j < places]
    return lax.ppermute(near, "space", inner), lax.ppermute(far, "space", outer)


def shards(guess, forcing, coarse_gain, kernel_levels, kernel_code, settle_levels, settle_class):
    intervals = lax.axis_size("tm")
    rows = guess.reshape(SLICES, C, PLANES, ROWS, 128).transpose(1, 2, 3, 0, 4).reshape(C * OWN * SLICES, 128)
    own, near, far, gain, kmat, speed = call(
        prep_kernel,
        [(rows, VMEM), (forcing, VMEM), (coarse_gain, VMEM)]
        + [(x, SMEM) for x in (kernel_levels, kernel_code, settle_levels, settle_class)],
        [arr(2 * C, OWN, 128), arr(2 * C, HALO, 128), arr(2 * C, HALO, 128), arr(intervals * PIECE, 128), arr(C, C), arr(C)],
        [VMEM] * 4 + [SMEM] * 2,
    )
    ops = [(kmat, SMEM), (speed, SMEM)]
    near, far = exchange(near, far)
    state, near, far, fwin = call(
        first_kernel,
        [(own, VMEM), (near, VMEM), (far, VMEM)] + ops,
        [arr(C, OWN, 128), arr(C, HALO, 128), arr(C, HALO, 128), arr(C, WIN, 128)],
        scratch=WORK,
    )
    near, far = exchange(near, far)
    shifted = lax.ppermute(state, "tm", [(i, i + 1) for i in range(intervals - 1)])
    (element,) = call(
        second_kernel,
        [(state, VMEM), (near, VMEM), (far, VMEM), (fwin, VMEM), (gain, VMEM)] + ops,
        [arr(intervals * PIECE, 128)],
        scratch=WORK,
    )
    pieces = lax.all_to_all(element.reshape(intervals, PIECE * 128), "tm", 0, 0, tiled=True)
    mine = lax.dynamic_slice_in_dim(gain.reshape(intervals, PIECE, 128), lax.axis_index("tm"), 1, axis=0)
    (sums,) = call(
        scan_kernel,
        [(pieces.reshape(intervals * PIECE, 128), VMEM), (mine, VMEM)],
        [arr(intervals * PIECE, 128)],
    )
    back = lax.all_to_all(sums.reshape(intervals, PIECE * 128), "tm", 0, 0, tiled=True)
    state, near, far, corr = call(
        gather_kernel,
        [(back.reshape(intervals * PIECE, 128), VMEM), (shifted, VMEM), (own, VMEM)],
        [arr(C, OWN, 128), arr(C, HALO, 128), arr(C, HALO, 128), arr(C * OWN, 128)],
    )
    near, far = exchange(near, far)
    (updated,) = call(
        last_kernel,
        [(state, VMEM), (near, VMEM), (far, VMEM), (fwin, VMEM)] + ops,
        [arr(C * OWN * SLICES, 128)],
        scratch=WORK,
    )
    updated = updated.reshape(C, PLANES, ROWS, SLICES, 128).transpose(3, 0, 1, 2, 4)
    return (
        updated.reshape(SLICES, C, PLANES, ROWS * 128),
        corr.reshape(1, C, PLANES, ROWS * 128),
    )


def solution(mesh):
    in_specs = (
        P("tm", None, "space", None),
        P(None, "space", None),
        P(None, "space", None),
        P(),
        P(),
        P(),
        P(),
    )
    out_specs = (P("tm", None, "space", None), P("tm", None, "space", None))
    return jax.shard_map(shards, mesh=mesh, in_specs=in_specs, out_specs=out_specs, check_vma=False)
```

```python
import functools

import jax
import jax.numpy as jnp
from jax import lax
from jax.experimental import pallas as pl
from jax.experimental.pallas import tpu as pltpu
from jax.sharding import PartitionSpec as P

F32 = jnp.float32
C = 12
NY = 16
NZ = 32
PLANES = 6
NX = 48
SLICES = 4
ROWS = 4
OWN = PLANES * ROWS
HALO = 4 * ROWS
THREE = 3 * ROWS
WIN = 64
BASE = 5 * ROWS
PIECE = 5
VMEM = pl.BlockSpec(memory_space=pltpu.VMEM)
SMEM = pl.BlockSpec(memory_space=pltpu.SMEM)
HBM = pl.BlockSpec(memory_space=pl.ANY)


def arr(*shape):
    return jax.ShapeDtypeStruct(shape, F32)


def even_place():
    return lax.axis_index("space") % 2 == 0


def put_sends(first, last, near, far):
    even = even_place()

    @pl.when(even)
    def _():
        last(near)
        first(far)

    @pl.when(jnp.logical_not(even))
    def _():
        first(near)
        last(far)


def put_halo(buf, near, far, count, start):
    even = even_place()

    def put(src, row):
        for c in range(C):
            buf[c, row : row + count, :] = src[start + c * count : start + (c + 1) * count, :]

    @pl.when(even)
    def _():
        put(far, BASE - count)
        put(near, BASE + OWN)

    @pl.when(jnp.logical_not(even))
    def _():
        put(near, BASE - count)
        put(far, BASE + OWN)


def pack(src, row, count, start):
    def into(dst):
        for c in range(C):
            dst[start + c * count : start + (c + 1) * count, :] = src[c, row : row + count, :]

    return into


def prep_kernel(guess, forcing, own, force, near, far, raw, fraw, sems):
    one = pltpu.make_async_copy(forcing, fraw, sems.at[0])
    two = pltpu.make_async_copy(guess, raw, sems.at[1])
    one.start()
    two.start()
    one.wait()
    for c in range(C):
        for r in range(ROWS):
            force[c, pl.ds(r, PLANES, stride=ROWS), :] = fraw[c, :, 128 * r : 128 * r + 128] * 0.1
    two.wait()
    for c in range(C):
        own[c] = raw[pl.ds(c * OWN * SLICES, OWN, stride=SLICES), :]

    def first(dst):
        pack(own, 0, HALO, 0)(dst)
        pack(force, 0, THREE, C * HALO)(dst)

    def last(dst):
        pack(own, OWN - HALO, HALO, 0)(dst)
        pack(force, OWN - THREE, THREE, C * HALO)(dst)

    put_sends(first, last, near, far)


def setup_kernel(raw, lv, cd, st, kl, gain_out, kv, wup, wfix, mask):
    for c in range(C):
        for r in range(ROWS):
            gain_out[pl.ds(c * OWN + r, PLANES, stride=ROWS), :] = raw[c, :, 128 * r : 128 * r + 128]
    gain_out[C * OWN :, :] = jnp.zeros((gain_out.shape[0] - C * OWN, 128), F32)
    lane = lax.broadcasted_iota(jnp.int32, (8, 128), 1)
    row = lax.broadcasted_iota(jnp.int32, (8, 128), 0)
    z = lane % NZ
    edge_row = row % ROWS
    for j in range(C):
        col = [lv[cd[i, j]] for i in range(C)]
        total = functools.reduce(lambda x, y: x + y, col)
        speed = st[kl[j]]
        for i in range(C):
            v = (col[i] - total) + (1.0 - 0.48) - speed if i == j else col[i]
            kv[i * C + j] = jnp.full((8, 128), v, F32)
        wup[j] = jnp.where(z < NZ - 1, 0.08 + speed, 0.0)
    wfix[0] = jnp.where(z > 0, F32(0.08), F32(0.0))
    wfix[1] = jnp.where(jnp.logical_and(lane >= 96, edge_row == ROWS - 1), F32(0.0), F32(0.08))
    wfix[2] = jnp.where(jnp.logical_and(lane < 32, edge_row == 0), F32(0.0), F32(0.08))
    start = lax.axis_index("space") * PLANES - 5
    for t in range(WIN // 8):
        plane = start + 2 * t + row // ROWS
        inside = jnp.logical_and(plane >= 0, plane < NX)
        mask[t] = jnp.where(inside, F32(1.0), F32(0.0))


def clear_edges(buf):
    z = jnp.zeros((C, 8, 128), F32)
    buf[:, 0:8, :] = z
    buf[:, WIN - 8 : WIN, :] = z


def block_step(src, dst, fwin, t, kv, wup, wfix, mask):
    lane = lax.broadcasted_iota(jnp.int32, (8, 128), 1)
    row = lax.broadcasted_iota(jnp.int32, (8, 128), 0)
    low = row < ROWS
    right = lane >= 96
    left = lane < 32
    wdn, wah, wbe = wfix[0], wfix[1], wfix[2]

    def rows(k):
        return pl.ds((t + k) * 8, 8)

    acc = []
    for i in range(C):
        p = [src[i, rows(k), :] for k in (-1, 0, 1, 2)]
        q = [pltpu.roll(v, 4, 0) for v in p]
        pair = []
        for k in (0, 1):
            c = p[k + 1]
            xs = q[k + 1] + jnp.where(low, q[k], q[k + 2])
            up = pltpu.roll(c, 127, 1)
            dn = pltpu.roll(c, 1, 1)
            ra = pltpu.roll(c, 96, 1)
            rb = pltpu.roll(c, 32, 1)
            ah = jnp.where(right, pltpu.roll(ra, 7, 0), ra)
            be = jnp.where(left, pltpu.roll(rb, 1, 0), rb)
            new = fwin[i, rows(k), :] + 0.08 * xs
            new = new + wup[i] * up
            new = new + wdn * dn
            new = new + wah * ah
            new = new + wbe * be
            pair.append(new)
        acc.append(pair)
    for j in range(C):
        c = [src[j, rows(k), :] for k in (0, 1)]
        for i in range(C):
            w = kv[i * C + j]
            acc[i] = [acc[i][k] + w * c[k] for k in (0, 1)]
    for k in (0, 1):
        m = mask[t + k]
        for i in range(C):
            dst[i, rows(k), :] = acc[i][k] * m


def steps(bufs, fwin, plan, coefs):
    for s, (first, count) in enumerate(plan):
        src, dst = bufs[s % 2], bufs[(s + 1) % 2]
        for b in range(count):
            block_step(src, dst, fwin, first + 2 * b, *coefs)


FOUR = ((1, 3), (1, 3), (2, 2), (2, 2))


def first_kernel(own, force, far, near, kv, wup, wfix, mask, state, send_near, send_far, fwin, a, b):
    clear_edges(a)
    clear_edges(b)
    clear_edges(fwin)
    a[:, BASE : BASE + OWN, :] = own[...]
    fwin[:, BASE : BASE + OWN, :] = force[...]
    put_halo(a, near, far, HALO, 0)
    put_halo(fwin, near, far, THREE, C * HALO)
    steps((a, b), fwin, FOUR, (kv, wup, wfix, mask))
    state[...] = a[:, BASE : BASE + OWN, :]
    put_sends(pack(state, 0, HALO, 0), pack(state, OWN - HALO, HALO, 0), send_near, send_far)


def second_kernel(state, far, near, fwin, gain, kv, wup, wfix, mask, out, a, b):
    clear_edges(a)
    clear_edges(b)
    a[:, BASE : BASE + OWN, :] = state[...]
    put_halo(a, near, far, HALO, 0)
    steps((a, b), fwin, FOUR, (kv, wup, wfix, mask))
    use = jnp.where(lax.axis_index("tm") > 0, F32(1.0), F32(0.0))
    for c in range(C):
        here = pl.ds(c * OWN, OWN)
        out[here, :] = a[c, BASE : BASE + OWN, :] - use * (gain[here, :] * state[c])
    out[C * OWN :, :] = jnp.zeros((out.shape[0] - C * OWN, 128), F32)


def scan_kernel(pieces, gain, out):
    count = pieces.shape[0] // PIECE
    mine = gain[0]
    running = pieces[0:PIECE, :]
    out[0 : 2 * PIECE, :] = jnp.zeros((2 * PIECE, 128), F32)
    for k in range(2, count):
        out[k * PIECE : (k + 1) * PIECE, :] = running
        if k + 1 < count:
            m = k - 1
            running = mine * running + pieces[m * PIECE : (m + 1) * PIECE, :]


def gather_kernel(pieces, one, own, state, near, far):
    k = lax.axis_index("tm")

    @pl.when(k == 0)
    def _():
        state[...] = own[...]

    @pl.when(k == 1)
    def _():
        state[...] = one[...]

    @pl.when(k >= 2)
    def _():
        for c in range(C):
            state[c] = pieces[c * OWN : (c + 1) * OWN, :]

    put_sends(pack(state, 0, THREE, 0), pack(state, OWN - THREE, THREE, 0), near, far)


def last_kernel(state, far, near, fwin, shifted, kv, wup, wfix, mask, out, corr, a, b):
    clear_edges(a)
    clear_edges(b)
    a[:, BASE : BASE + OWN, :] = state[...]
    put_halo(a, near, far, THREE, 0)

    def emit(buf, j):
        for c in range(C):
            out[pl.ds(c * OWN * SLICES + j, OWN, stride=SLICES), :] = buf[c, BASE : BASE + OWN, :]

    emit(a, 0)
    bufs = (a, b)
    for j, one in enumerate(((1, 3), (2, 2), (2, 2))):
        src, dst = bufs[j % 2], bufs[(j + 1) % 2]
        steps((src, dst), fwin, (one,), (kv, wup, wfix, mask))
        emit(dst, j + 1)
    late = lax.axis_index("tm") >= 2
    for c in range(C):
        corr[c * OWN : (c + 1) * OWN, :] = jnp.where(late, state[c] - shifted[c], 0.0)


WORK = [pltpu.VMEM((C, WIN, 128), F32), pltpu.VMEM((C, WIN, 128), F32)]


def call(kernel, ins, outs, scratch=(), place=None, grant=32):
    return pl.pallas_call(
        kernel,
        out_shape=outs,
        in_specs=place or [VMEM] * len(ins),
        out_specs=[VMEM] * len(outs),
        scratch_shapes=list(scratch),
        compiler_params=pltpu.CompilerParams(vmem_limit_bytes=grant * 1024 * 1024),
        name=kernel.__name__,
    )(*ins)


def exchange(near, far):
    places = lax.axis_size("space")
    inner = [(i, i ^ 1) for i in range(places)]
    outer = [(i, j) for i in range(places) for j in [i - 1 if i % 2 == 0 else i + 1] if 0 <= j < places]
    far = lax.ppermute(far, "space", outer)
    near = lax.ppermute(near, "space", inner)
    return near, far


def shards(guess, forcing, coarse_gain, kernel_levels, kernel_code, settle_levels, settle_class):
    intervals = lax.axis_size("tm")
    rows = guess.reshape(SLICES, C, PLANES, ROWS, 128).transpose(1, 2, 3, 0, 4).reshape(C * OWN * SLICES, 128)
    slab = arr(C, OWN, 128)
    wide, four, three = (arr(C * n, 128) for n in (HALO + THREE, HALO, THREE))
    pieces = arr(intervals * PIECE, 128)
    own, force, near, far = call(
        prep_kernel,
        [rows, forcing],
        [slab, slab, wide, wide],
        [pltpu.VMEM(rows.shape, F32), pltpu.VMEM(forcing.shape, F32), pltpu.SemaphoreType.DMA((2,))],
        [HBM] * 2,
        60,
    )
    near, far = exchange(near, far)
    small = (kernel_levels, kernel_code, settle_levels, settle_class)
    gain, *coefs = call(
        setup_kernel,
        [coarse_gain, *small],
        [pieces, arr(C * C, 8, 128), arr(C, 8, 128), arr(3, 8, 128), arr(WIN // 8, 8, 128)],
        place=[VMEM] + [SMEM] * len(small),
    )
    mine = lax.dynamic_slice_in_dim(gain.reshape(intervals, PIECE, 128), lax.axis_index("tm"), 1, axis=0)
    state, near, far, fwin = call(
        first_kernel, [own, force, far, near, *coefs], [slab, four, four, arr(C, WIN, 128)], WORK
    )
    near, far = exchange(near, far)
    one = lax.ppermute(state, "tm", [(0, 1)])
    shifted = lax.ppermute(state, "tm", [(i, i + 1) for i in range(1, intervals - 1)])
    (element,) = call(second_kernel, [state, far, near, fwin, gain, *coefs], [pieces], WORK)
    spread = lax.all_to_all(element.reshape(intervals, PIECE * 128), "tm", 0, 0, tiled=True)
    (sums,) = call(scan_kernel, [spread.reshape(intervals * PIECE, 128), mine], [pieces])
    back = lax.all_to_all(sums.reshape(intervals, PIECE * 128), "tm", 0, 0, tiled=True)
    state, near, far = call(
        gather_kernel, [back.reshape(intervals * PIECE, 128), one, own], [slab, three, three]
    )
    near, far = exchange(near, far)
    updated, corr = call(
        last_kernel,
        [state, far, near, fwin, shifted, *coefs],
        [arr(C * OWN * SLICES, 128), arr(C * OWN, 128)],
        WORK,
    )
    updated = updated.reshape(C, PLANES, ROWS, SLICES, 128).transpose(3, 0, 1, 2, 4)
    return (
        updated.reshape(SLICES, C, PLANES, ROWS * 128),
        corr.reshape(1, C, PLANES, ROWS * 128),
    )


def solution(mesh):
    in_specs = (
        P("tm", None, "space", None),
        P(None, "space", None),
        P(None, "space", None),
        P(),
        P(),
        P(),
        P(),
    )
    out_specs = (P("tm", None, "space", None), P("tm", None, "space", None))
    return jax.shard_map(shards, mesh=mesh, in_specs=in_specs, out_specs=out_specs, check_vma=False)
```

```python
import functools

import jax
import jax.numpy as jnp
from jax import lax
from jax.experimental import pallas as pl
from jax.experimental.pallas import tpu as pltpu
from jax.sharding import PartitionSpec as P

F32 = jnp.float32
C = 12
NY = 16
NZ = 32
PLANES = 6
NX = 48
SLICES = 4
ROWS = 4
OWN = PLANES * ROWS
HALO = 4 * ROWS
THREE = 3 * ROWS
WIN = 64
BASE = 5 * ROWS
GROUP = 8
PIECE = 40
VMEM = pl.BlockSpec(memory_space=pltpu.VMEM)
SMEM = pl.BlockSpec(memory_space=pltpu.SMEM)
HBM = pl.BlockSpec(memory_space=pl.ANY)


def arr(*shape):
    return jax.ShapeDtypeStruct(shape, F32)


def even_place():
    return lax.axis_index("space") % 2 == 0


def put_sends(first, last, near, far):
    even = even_place()

    @pl.when(even)
    def _():
        last(near)
        first(far)

    @pl.when(jnp.logical_not(even))
    def _():
        first(near)
        last(far)


def put_halo(buf, near, far, count, start):
    even = even_place()

    def put(src, row):
        for c in range(C):
            buf[c, row : row + count, :] = src[start + c * count : start + (c + 1) * count, :]

    @pl.when(even)
    def _():
        put(far, BASE - count)
        put(near, BASE + OWN)

    @pl.when(jnp.logical_not(even))
    def _():
        put(near, BASE - count)
        put(far, BASE + OWN)


def pack(src, row, count, start, base=0):
    def into(dst):
        for c in range(C):
            dst[start + c * count : start + (c + 1) * count, :] = src[base + c, row : row + count, :]

    return into


def take_guess(raw, both):
    for c in range(C):
        both[c] = raw[pl.ds(c * OWN * SLICES, OWN, stride=SLICES), :]


def take_forcing(raw, both):
    for c in range(C):
        for r in range(ROWS):
            both[C + c, pl.ds(r, PLANES, stride=ROWS), :] = raw[c, :, 128 * r : 128 * r + 128] * 0.1


def prep_kernel(guess, forcing, near, far, both, raw, fraw, sems):
    one = pltpu.make_async_copy(forcing, fraw, sems.at[0])
    two = pltpu.make_async_copy(guess, raw, sems.at[1])
    one.start()
    two.start()
    one.wait()
    take_forcing(fraw, both)
    two.wait()
    take_guess(raw, both)

    def first(dst):
        pack(both, 0, HALO, 0)(dst)
        pack(both, 0, THREE, C * HALO, C)(dst)

    def last(dst):
        pack(both, OWN - HALO, HALO, 0)(dst)
        pack(both, OWN - THREE, THREE, C * HALO, C)(dst)

    put_sends(first, last, near, far)


def setup_kernel(guess, forcing, raw, lv, cd, st, kl, both, gain_out, kv, wup, wfix, mask):
    take_guess(guess, both)
    take_forcing(forcing, both)
    for c in range(C):
        for r in range(ROWS):
            gain_out[pl.ds(c * OWN + r, PLANES, stride=ROWS), :] = raw[c, :, 128 * r : 128 * r + 128]
    gain_out[C * OWN :, :] = jnp.zeros((gain_out.shape[0] - C * OWN, 128), F32)
    lane = lax.broadcasted_iota(jnp.int32, (8, 128), 1)
    row = lax.broadcasted_iota(jnp.int32, (8, 128), 0)
    z = lane % NZ
    edge_row = row % ROWS
    for j in range(C):
        col = [lv[cd[i, j]] for i in range(C)]
        total = functools.reduce(lambda x, y: x + y, col)
        speed = st[kl[j]]
        for i in range(C):
            v = (col[i] - total) + (1.0 - 0.48) - speed if i == j else col[i]
            kv[i * C + j] = jnp.full((8, 128), v, F32)
        wup[j] = jnp.where(z < NZ - 1, 0.08 + speed, 0.0)
    wfix[0] = jnp.where(z > 0, F32(0.08), F32(0.0))
    wfix[1] = jnp.where(jnp.logical_and(lane >= 96, edge_row == ROWS - 1), F32(0.0), F32(0.08))
    wfix[2] = jnp.where(jnp.logical_and(lane < 32, edge_row == 0), F32(0.0), F32(0.08))
    start = lax.axis_index("space") * PLANES - 5
    for t in range(WIN // 8):
        plane = start + 2 * t + row // ROWS
        inside = jnp.logical_and(plane >= 0, plane < NX)
        mask[t] = jnp.where(inside, F32(1.0), F32(0.0))


def clear_edges(buf):
    z = jnp.zeros((C, 8, 128), F32)
    buf[:, 0:8, :] = z
    buf[:, WIN - 8 : WIN, :] = z


def block_step(src, dst, fwin, t, kv, wup, wfix, mask):
    lane = lax.broadcasted_iota(jnp.int32, (8, 128), 1)
    row = lax.broadcasted_iota(jnp.int32, (8, 128), 0)
    low = row < ROWS
    right = lane >= 96
    left = lane < 32
    wdn, wah, wbe = wfix[0], wfix[1], wfix[2]

    def rows(k):
        return pl.ds((t + k) * 8, 8)

    acc = []
    for i in range(C):
        p = [src[i, rows(k), :] for k in (-1, 0, 1, 2)]
        q = [pltpu.roll(v, 4, 0) for v in p]
        pair = []
        for k in (0, 1):
            c = p[k + 1]
            xs = q[k + 1] + jnp.where(low, q[k], q[k + 2])
            up = pltpu.roll(c, 127, 1)
            dn = pltpu.roll(c, 1, 1)
            ra = pltpu.roll(c, 96, 1)
            rb = pltpu.roll(c, 32, 1)
            ah = jnp.where(right, pltpu.roll(ra, 7, 0), ra)
            be = jnp.where(left, pltpu.roll(rb, 1, 0), rb)
            new = fwin[i, rows(k), :] + 0.08 * xs
            new = new + wup[i] * up
            new = new + wdn * dn
            new = new + wah * ah
            new = new + wbe * be
            pair.append(new)
        acc.append(pair)
    for j in range(C):
        c = [src[j, rows(k), :] for k in (0, 1)]
        for i in range(C):
            w = kv[i * C + j]
            acc[i] = [acc[i][k] + w * c[k] for k in (0, 1)]
    for k in (0, 1):
        m = mask[t + k]
        for i in range(C):
            dst[i, rows(k), :] = acc[i][k] * m


def steps(bufs, fwin, plan, coefs):
    for s, (first, count) in enumerate(plan):
        src, dst = bufs[s % 2], bufs[(s + 1) % 2]
        for b in range(count):
            block_step(src, dst, fwin, first + 2 * b, *coefs)


FOUR = ((1, 3), (1, 3), (2, 2), (2, 2))


def first_kernel(both, far, near, kv, wup, wfix, mask, state, send_near, send_far, fwin, a, b):
    clear_edges(a)
    clear_edges(b)
    clear_edges(fwin)
    a[:, BASE : BASE + OWN, :] = both[:C]
    fwin[:, BASE : BASE + OWN, :] = both[C:]
    put_halo(a, near, far, HALO, 0)
    put_halo(fwin, near, far, THREE, C * HALO)
    steps((a, b), fwin, FOUR, (kv, wup, wfix, mask))
    state[...] = a[:, BASE : BASE + OWN, :]
    put_sends(pack(state, 0, HALO, 0), pack(state, OWN - HALO, HALO, 0), send_near, send_far)


def second_kernel(state, far, near, fwin, gain, kv, wup, wfix, mask, out, a, b):
    clear_edges(a)
    clear_edges(b)
    a[:, BASE : BASE + OWN, :] = state[...]
    put_halo(a, near, far, HALO, 0)
    steps((a, b), fwin, FOUR, (kv, wup, wfix, mask))
    use = jnp.where(lax.axis_index("tm") > 0, F32(1.0), F32(0.0))
    for c in range(C):
        here = pl.ds(c * OWN, OWN)
        out[here, :] = a[c, BASE : BASE + OWN, :] - use * (gain[here, :] * state[c])
    out[C * OWN :, :] = jnp.zeros((out.shape[0] - C * OWN, 128), F32)


def my_gain(gain):
    place = lax.axis_index("tm") % GROUP
    return gain[pl.ds(pl.multiple_of(place * PIECE, 8), PIECE), :]


def slot(i):
    return slice(i * PIECE, (i + 1) * PIECE)


def local_kernel(pieces, gain, sums, total, short):
    mine = my_gain(gain)
    running = pieces[slot(0), :]
    sums[slot(0), :] = running
    for i in range(1, GROUP):
        running = mine * running + pieces[slot(i), :]
        sums[slot(i), :] = running
        if i == GROUP - 2:
            short[...] = running
    for i in range(GROUP):
        total[slot(i), :] = running


def prefix_kernel(totals, short, sums, gain, out):
    group = lax.axis_index("tm") // GROUP
    g1 = my_gain(gain)
    g2 = g1 * g1
    g4 = g2 * g2
    g8 = g4 * g4
    before = jnp.zeros((PIECE, 128), F32)
    ahead = before
    for g in range(GROUP - 1):
        take = g < group
        ahead = jnp.where(take, before, ahead)
        before = jnp.where(take, g8 * before + totals[slot(g), :], before)
    out[slot(0), :] = short[...] + (g4 * g2 * g1) * ahead
    out[slot(1), :] = before
    for i in range(2, GROUP):
        before = g1 * before
        out[slot(i), :] = sums[slot(i - 2), :] + before


def gather_kernel(pieces, one, both, state, near, far):
    k = lax.axis_index("tm")

    @pl.when(k == 0)
    def _():
        state[...] = both[:C]

    @pl.when(k == 1)
    def _():
        state[...] = one[...]

    @pl.when(k >= 2)
    def _():
        for c in range(C):
            state[c] = pieces[c * OWN : (c + 1) * OWN, :]

    put_sends(pack(state, 0, THREE, 0), pack(state, OWN - THREE, THREE, 0), near, far)


def last_kernel(state, far, near, fwin, shifted, kv, wup, wfix, mask, out, corr, a, b):
    clear_edges(a)
    clear_edges(b)
    a[:, BASE : BASE + OWN, :] = state[...]
    put_halo(a, near, far, THREE, 0)

    def emit(buf, j):
        for c in range(C):
            out[pl.ds(c * OWN * SLICES + j, OWN, stride=SLICES), :] = buf[c, BASE : BASE + OWN, :]

    emit(a, 0)
    bufs = (a, b)
    for j, one in enumerate(((1, 3), (2, 2), (2, 2))):
        src, dst = bufs[j % 2], bufs[(j + 1) % 2]
        steps((src, dst), fwin, (one,), (kv, wup, wfix, mask))
        emit(dst, j + 1)
    late = lax.axis_index("tm") >= 2
    for c in range(C):
        corr[c * OWN : (c + 1) * OWN, :] = jnp.where(late, state[c] - shifted[c], 0.0)


WORK = [pltpu.VMEM((C, WIN, 128), F32), pltpu.VMEM((C, WIN, 128), F32)]


def call(kernel, ins, outs, scratch=(), place=None, grant=32):
    return pl.pallas_call(
        kernel,
        out_shape=outs,
        in_specs=place or [VMEM] * len(ins),
        out_specs=[VMEM] * len(outs),
        scratch_shapes=list(scratch),
        compiler_params=pltpu.CompilerParams(vmem_limit_bytes=grant * 1024 * 1024),
        name=kernel.__name__,
    )(*ins)


def exchange(near, far):
    places = lax.axis_size("space")
    inner = [(i, i ^ 1) for i in range(places)]
    outer = [(i, j) for i in range(places) for j in [i - 1 if i % 2 == 0 else i + 1] if 0 <= j < places]
    far = lax.ppermute(far, "space", outer)
    near = lax.ppermute(near, "space", inner)
    return near, far


def swap(value, stride):
    count = lax.axis_size("tm")
    firsts = [i for i in range(count) if (i // stride) % GROUP == 0]
    groups = [[i + stride * j for j in range(GROUP)] for i in firsts]
    slots = value.reshape(GROUP, PIECE, 128)
    return lax.all_to_all(slots, "tm", 0, 0, tiled=True, axis_index_groups=groups).reshape(value.shape)


def shards(guess, forcing, coarse_gain, kernel_levels, kernel_code, settle_levels, settle_class):
    intervals = lax.axis_size("tm")
    rows = guess.reshape(SLICES, C, PLANES, ROWS, 128).transpose(1, 2, 3, 0, 4).reshape(C * OWN * SLICES, 128)
    slab = arr(C, OWN, 128)
    wide, four, three = (arr(C * n, 128) for n in (HALO + THREE, HALO, THREE))
    pieces = arr(GROUP * PIECE, 128)
    near, far = call(
        prep_kernel,
        [rows, forcing],
        [wide, wide],
        [pltpu.VMEM((2 * C, OWN, 128), F32), pltpu.VMEM(rows.shape, F32), pltpu.VMEM(forcing.shape, F32), pltpu.SemaphoreType.DMA((2,))],
        [HBM] * 2,
        60,
    )
    near, far = exchange(near, far)
    small = (kernel_levels, kernel_code, settle_levels, settle_class)
    both, gain, *coefs = call(
        setup_kernel,
        [rows, forcing, coarse_gain, *small],
        [arr(2 * C, OWN, 128), pieces, arr(C * C, 8, 128), arr(C, 8, 128), arr(3, 8, 128), arr(WIN // 8, 8, 128)],
        place=[VMEM] * 3 + [SMEM] * len(small),
    )
    state, near, far, fwin = call(
        first_kernel, [both, far, near, *coefs], [slab, four, four, arr(C, WIN, 128)], WORK
    )
    near, far = exchange(near, far)
    one = lax.ppermute(state, "tm", [(0, 1)])
    shifted = lax.ppermute(state, "tm", [(i, i + 1) for i in range(1, intervals - 1)])
    (element,) = call(second_kernel, [state, far, near, fwin, gain, *coefs], [pieces], WORK)
    spread = swap(element, 1)
    sums, totals, short = call(local_kernel, [spread, gain], [pieces, pieces, arr(PIECE, 128)])
    totals = swap(totals, GROUP)
    short = lax.ppermute(short, "tm", [(i, i + GROUP) for i in range(intervals - GROUP)])
    (back,) = call(prefix_kernel, [totals, short, sums, gain], [pieces])
    back = swap(back, 1)
    state, near, far = call(
        gather_kernel, [back, one, both], [slab, three, three]
    )
    near, far = exchange(near, far)
    updated, corr = call(
        last_kernel,
        [state, far, near, fwin, shifted, *coefs],
        [arr(C * OWN * SLICES, 128), arr(C * OWN, 128)],
        WORK,
    )
    updated = updated.reshape(C, PLANES, ROWS, SLICES, 128).transpose(3, 0, 1, 2, 4)
    return (
        updated.reshape(SLICES, C, PLANES, ROWS * 128),
        corr.reshape(1, C, PLANES, ROWS * 128),
    )


def solution(mesh):
    in_specs = (
        P("tm", None, "space", None),
        P(None, "space", None),
        P(None, "space", None),
        P(),
        P(),
        P(),
        P(),
    )
    out_specs = (P("tm", None, "space", None), P("tm", None, "space", None))
    return jax.shard_map(shards, mesh=mesh, in_specs=in_specs, out_specs=out_specs, check_vma=False)
```

```python
import functools

import jax
import jax.numpy as jnp
from jax import lax
from jax.experimental import pallas as pl
from jax.experimental.pallas import tpu as pltpu
from jax.sharding import PartitionSpec as P

F32 = jnp.float32
C = 12
HALF = C // 2
NY = 16
NZ = 32
PLANES = 6
NX = 48
SLICES = 4
ROWS = 4
OWN = PLANES * ROWS
HALO = 4 * ROWS
THREE = 3 * ROWS
WIN = 64
BASE = 5 * ROWS
GROUP = 8
PIECE = 40
VMEM = pl.BlockSpec(memory_space=pltpu.VMEM)
SMEM = pl.BlockSpec(memory_space=pltpu.SMEM)
HBM = pl.BlockSpec(memory_space=pl.ANY)


def arr(*shape):
    return jax.ShapeDtypeStruct(shape, F32)


def even_place():
    return lax.axis_index("space") % 2 == 0


def put_sends(first, last, near, far):
    even = even_place()

    @pl.when(even)
    def _():
        last(near)
        first(far)

    @pl.when(jnp.logical_not(even))
    def _():
        first(near)
        last(far)


def put_halo(buf, near, far, count, start):
    even = even_place()

    def put(src, row):
        for c in range(C):
            buf[c, row : row + count, :] = src[start + c * count : start + (c + 1) * count, :]

    @pl.when(even)
    def _():
        put(far, BASE - count)
        put(near, BASE + OWN)

    @pl.when(jnp.logical_not(even))
    def _():
        put(near, BASE - count)
        put(far, BASE + OWN)


def pack(src, row, count, start):
    def into(dst):
        for c in range(C):
            dst[start + c * count : start + (c + 1) * count, :] = src[c, row : row + count, :]

    return into


def take_guess(raw, own):
    for c in range(C):
        own[c] = raw[pl.ds(c * OWN * SLICES, OWN, stride=SLICES), :]


def take_forcing(raw, force):
    for c in range(C):
        for r in range(ROWS):
            force[c, pl.ds(r, PLANES, stride=ROWS), :] = raw[c, :, 128 * r : 128 * r + 128] * 0.1


def prep_kernel(guess, forcing, near, far, own, force, raw, fraw, sems):
    one = pltpu.make_async_copy(forcing, fraw, sems.at[0])
    two = pltpu.make_async_copy(guess, raw, sems.at[1])
    one.start()
    two.start()
    one.wait()
    take_forcing(fraw, force)
    two.wait()
    take_guess(raw, own)

    def first(dst):
        pack(own, 0, HALO, 0)(dst)
        pack(force, 0, THREE, C * HALO)(dst)

    def last(dst):
        pack(own, OWN - HALO, HALO, 0)(dst)
        pack(force, OWN - THREE, THREE, C * HALO)(dst)

    put_sends(first, last, near, far)


def gain_kernel(raw, gain_out):
    for c in range(C):
        for r in range(ROWS):
            gain_out[pl.ds(c * OWN + r, PLANES, stride=ROWS), :] = raw[c, :, 128 * r : 128 * r + 128]
    gain_out[C * OWN :, :] = jnp.zeros((gain_out.shape[0] - C * OWN, 128), F32)


def setup_kernel(forcing, lv, cd, st, kl, force, kv, wup, wfix, mask):
    take_forcing(forcing, force)
    lane = lax.broadcasted_iota(jnp.int32, (8, 128), 1)
    row = lax.broadcasted_iota(jnp.int32, (8, 128), 0)
    z = lane % NZ
    edge_row = row % ROWS
    for j in range(C):
        col = [lv[cd[i, j]] for i in range(C)]
        total = functools.reduce(lambda x, y: x + y, col)
        speed = st[kl[j]]
        for i in range(C):
            v = (col[i] - total) + (1.0 - 0.48) - speed if i == j else col[i]
            kv[i * C + j] = jnp.full((8, 128), v, F32)
        wup[j] = jnp.where(z < NZ - 1, 0.08 + speed, 0.0)
    wfix[0] = jnp.where(z > 0, F32(0.08), F32(0.0))
    wfix[1] = jnp.where(jnp.logical_and(lane >= 96, edge_row == ROWS - 1), F32(0.0), F32(0.08))
    wfix[2] = jnp.where(jnp.logical_and(lane < 32, edge_row == 0), F32(0.0), F32(0.08))
    start = lax.axis_index("space") * PLANES - 5
    for t in range(WIN // 8):
        plane = start + 2 * t + row // ROWS
        inside = jnp.logical_and(plane >= 0, plane < NX)
        mask[t] = jnp.where(inside, F32(1.0), F32(0.0))


def clear_edges(buf):
    z = jnp.zeros((C, 8, 128), F32)
    buf[:, 0:8, :] = z
    buf[:, WIN - 8 : WIN, :] = z


def block_step(src, dst, fwin, t, kv, wup, wfix, mask):
    lane = lax.broadcasted_iota(jnp.int32, (8, 128), 1)
    row = lax.broadcasted_iota(jnp.int32, (8, 128), 0)
    low = row < ROWS
    right = lane >= 96
    left = lane < 32
    wdn, wah, wbe = wfix[0], wfix[1], wfix[2]

    def rows(k):
        return pl.ds((t + k) * 8, 8)

    acc = []
    for i in range(C):
        p = [src[i, rows(k), :] for k in (-1, 0, 1, 2)]
        q = [pltpu.roll(v, 4, 0) for v in p]
        pair = []
        for k in (0, 1):
            c = p[k + 1]
            xs = q[k + 1] + jnp.where(low, q[k], q[k + 2])
            up = pltpu.roll(c, 127, 1)
            dn = pltpu.roll(c, 1, 1)
            ra = pltpu.roll(c, 96, 1)
            rb = pltpu.roll(c, 32, 1)
            ah = jnp.where(right, pltpu.roll(ra, 7, 0), ra)
            be = jnp.where(left, pltpu.roll(rb, 1, 0), rb)
            new = fwin[i, rows(k), :] + 0.08 * xs
            new = new + wup[i] * up
            new = new + wdn * dn
            new = new + wah * ah
            new = new + wbe * be
            pair.append(new)
        acc.append(pair)
    for j in range(C):
        c = [src[j, rows(k), :] for k in (0, 1)]
        for i in range(C):
            w = kv[i * C + j]
            acc[i] = [acc[i][k] + w * c[k] for k in (0, 1)]
    for k in (0, 1):
        m = mask[t + k]
        for i in range(C):
            dst[i, rows(k), :] = acc[i][k] * m


def steps(bufs, fwin, plan, coefs):
    for s, (first, count) in enumerate(plan):
        src, dst = bufs[s % 2], bufs[(s + 1) % 2]
        for b in range(count):
            block_step(src, dst, fwin, first + 2 * b, *coefs)


FOUR = ((1, 3), (1, 3), (2, 2), (2, 2))


def first_kernel(guess, force, far, near, kv, wup, wfix, mask, own, state, low, high, send_near, send_far, fwin, a, b):
    clear_edges(a)
    clear_edges(b)
    clear_edges(fwin)
    take_guess(guess, own)
    a[:, BASE : BASE + OWN, :] = own[...]
    fwin[:, BASE : BASE + OWN, :] = force[...]
    put_halo(a, near, far, HALO, 0)
    put_halo(fwin, near, far, THREE, C * HALO)
    steps((a, b), fwin, FOUR, (kv, wup, wfix, mask))
    state[...] = a[:, BASE : BASE + OWN, :]
    low[...] = a[:HALF, BASE : BASE + OWN, :]
    high[...] = a[HALF:, BASE : BASE + OWN, :]
    put_sends(pack(state, 0, HALO, 0), pack(state, OWN - HALO, HALO, 0), send_near, send_far)


def second_kernel(state, far, near, fwin, gain, kv, wup, wfix, mask, out, a, b):
    clear_edges(a)
    clear_edges(b)
    a[:, BASE : BASE + OWN, :] = state[...]
    put_halo(a, near, far, HALO, 0)
    steps((a, b), fwin, FOUR, (kv, wup, wfix, mask))
    use = jnp.where(lax.axis_index("tm") > 0, F32(1.0), F32(0.0))
    for c in range(C):
        here = pl.ds(c * OWN, OWN)
        out[here, :] = a[c, BASE : BASE + OWN, :] - use * (gain[here, :] * state[c])
    out[C * OWN :, :] = jnp.zeros((out.shape[0] - C * OWN, 128), F32)


def my_gain(gain):
    place = GROUP - 1 - lax.axis_index("tm") % GROUP
    return gain[pl.ds(pl.multiple_of(place * PIECE, 8), PIECE), :]


def slot(i):
    return slice((GROUP - 1 - i) * PIECE, (GROUP - i) * PIECE)


def local_kernel(pieces, gain, sums, total, short):
    mine = my_gain(gain)
    running = pieces[slot(0), :]
    sums[slot(0), :] = running
    for i in range(1, GROUP):
        running = mine * running + pieces[slot(i), :]
        sums[slot(i), :] = running
        if i == GROUP - 2:
            short[...] = running
    for i in range(GROUP):
        total[slot(i), :] = running


def prefix_kernel(totals, cross, shifted, short, sums, gain, out):
    del cross, shifted
    group = lax.axis_index("tm") // GROUP
    g1 = my_gain(gain)
    g2 = g1 * g1
    g4 = g2 * g2
    g8 = g4 * g4
    before = jnp.zeros((PIECE, 128), F32)
    ahead = before
    for g in range(GROUP - 1):
        take = g < group
        ahead = jnp.where(take, before, ahead)
        before = jnp.where(take, g8 * before + totals[slot(g), :], before)
    out[slot(0), :] = short[...] + (g4 * g2 * g1) * ahead
    out[slot(1), :] = before
    for i in range(2, GROUP):
        before = g1 * before
        out[slot(i), :] = sums[slot(i - 2), :] + before


def gather_kernel(pieces, one, own, state, near, far):
    k = lax.axis_index("tm")

    @pl.when(k == 0)
    def _():
        state[...] = own[...]

    @pl.when(k == 1)
    def _():
        state[...] = one[...]

    @pl.when(k >= 2)
    def _():
        for c in range(C):
            state[c] = pieces[c * OWN : (c + 1) * OWN, :]

    put_sends(pack(state, 0, THREE, 0), pack(state, OWN - THREE, THREE, 0), near, far)


def last_kernel(state, far, near, fwin, shifted, cross, rest, kv, wup, wfix, mask, out, corr, a, b):
    clear_edges(a)
    clear_edges(b)
    a[:, BASE : BASE + OWN, :] = state[...]
    put_halo(a, near, far, THREE, 0)

    def emit(buf, j):
        for c in range(C):
            out[pl.ds(c * OWN * SLICES + j, OWN, stride=SLICES), :] = buf[c, BASE : BASE + OWN, :]

    emit(a, 0)
    bufs = (a, b)
    for j, one in enumerate(((1, 3), (2, 2), (2, 2))):
        src, dst = bufs[j % 2], bufs[(j + 1) % 2]
        steps((src, dst), fwin, (one,), (kv, wup, wfix, mask))
        emit(dst, j + 1)
    late = lax.axis_index("tm") >= 2
    for c in range(C):
        over = cross[c] if c < HALF else rest[c - HALF]
        corr[c * OWN : (c + 1) * OWN, :] = jnp.where(late, state[c] - (shifted[c] + over), 0.0)


WORK = [pltpu.VMEM((C, WIN, 128), F32), pltpu.VMEM((C, WIN, 128), F32)]


def call(kernel, ins, outs, scratch=(), place=None, grant=32):
    return pl.pallas_call(
        kernel,
        out_shape=outs,
        in_specs=place or [VMEM] * len(ins),
        out_specs=[VMEM] * len(outs),
        scratch_shapes=list(scratch),
        compiler_params=pltpu.CompilerParams(vmem_limit_bytes=grant * 1024 * 1024),
        name=kernel.__name__,
    )(*ins)


def exchange(near, far):
    places = lax.axis_size("space")
    inner = [(i, i ^ 1) for i in range(places)]
    outer = [(i, j) for i in range(places) for j in [i - 1 if i % 2 == 0 else i + 1] if 0 <= j < places]
    far = lax.ppermute(far, "space", outer)
    near = lax.ppermute(near, "space", inner)
    return near, far


def swap(value, stride):
    count = lax.axis_size("tm")
    firsts = [i for i in range(count) if (i // stride) % GROUP == 0]
    groups = [[i + stride * j for j in reversed(range(GROUP))] for i in firsts]
    slots = value.reshape(GROUP, PIECE, 128)
    return lax.all_to_all(slots, "tm", 0, 0, tiled=True, axis_index_groups=groups).reshape(value.shape)


def shards(guess, forcing, coarse_gain, kernel_levels, kernel_code, settle_levels, settle_class):
    intervals = lax.axis_size("tm")
    rows = guess.reshape(SLICES, C, PLANES, ROWS, 128).transpose(1, 2, 3, 0, 4).reshape(C * OWN * SLICES, 128)
    slab = arr(C, OWN, 128)
    wide, four, three = (arr(C * n, 128) for n in (HALO + THREE, HALO, THREE))
    pieces = arr(GROUP * PIECE, 128)
    near, far = call(
        prep_kernel,
        [rows, forcing],
        [wide, wide],
        [pltpu.VMEM(slab.shape, F32), pltpu.VMEM(slab.shape, F32), pltpu.VMEM(rows.shape, F32), pltpu.VMEM(forcing.shape, F32), pltpu.SemaphoreType.DMA((2,))],
        [HBM] * 2,
        60,
    )
    near, far = exchange(near, far)
    small = (kernel_levels, kernel_code, settle_levels, settle_class)
    force, *coefs = call(
        setup_kernel,
        [forcing, *small],
        [slab, arr(C * C, 8, 128), arr(C, 8, 128), arr(3, 8, 128), arr(WIN // 8, 8, 128)],
        place=[VMEM] + [SMEM] * len(small),
    )
    (gain,) = call(gain_kernel, [coarse_gain], [pieces])
    half = arr(HALF, OWN, 128)
    own, state, low, high, near, far, fwin = call(
        first_kernel,
        [rows, force, far, near, *coefs],
        [slab, slab, half, half, four, four, arr(C, WIN, 128)],
        WORK,
    )
    near, far = exchange(near, far)
    middle = intervals // 2
    shifted = lax.ppermute(state, "tm", [(i, i + 1) for i in range(intervals - 1) if i + 1 != middle])
    cross = lax.ppermute(low, "tm", [(middle - 1, middle)])
    rest = lax.ppermute(high, "tm", [(middle - 1, middle)])
    (element,) = call(second_kernel, [state, far, near, fwin, gain, *coefs], [pieces], WORK)
    spread = swap(element, 1)
    sums, totals, short = call(local_kernel, [spread, gain], [pieces, pieces, arr(PIECE, 128)])
    totals = swap(totals, GROUP)
    short = lax.ppermute(short, "tm", [(i, i + GROUP) for i in range(intervals - GROUP)])
    (back,) = call(prefix_kernel, [totals, cross, shifted, short, sums, gain], [pieces])
    back = swap(back, 1)
    state, near, far = call(
        gather_kernel, [back, shifted, own], [slab, three, three]
    )
    near, far = exchange(near, far)
    updated, corr = call(
        last_kernel,
        [state, far, near, fwin, shifted, cross, rest, *coefs],
        [arr(C * OWN * SLICES, 128), arr(C * OWN, 128)],
        WORK,
    )
    updated = updated.reshape(C, PLANES, ROWS, SLICES, 128).transpose(3, 0, 1, 2, 4)
    return (
        updated.reshape(SLICES, C, PLANES, ROWS * 128),
        corr.reshape(1, C, PLANES, ROWS * 128),
    )


def solution(mesh):
    in_specs = (
        P("tm", None, "space", None),
        P(None, "space", None),
        P(None, "space", None),
        P(),
        P(),
        P(),
        P(),
    )
    out_specs = (P("tm", None, "space", None), P("tm", None, "space", None))
    return jax.shard_map(shards, mesh=mesh, in_specs=in_specs, out_specs=out_specs, check_vma=False)
```

```python
import functools

import jax
import jax.numpy as jnp
from jax import lax
from jax.experimental import pallas as pl
from jax.experimental.pallas import tpu as pltpu
from jax.sharding import PartitionSpec as P

F32 = jnp.float32
C = 12
NY = 16
NZ = 32
PLANES = 6
NX = 48
SLICES = 4
ROWS = 4
OWN = PLANES * ROWS
HALO = 4 * ROWS
THREE = 3 * ROWS
WIN = 64
BASE = 5 * ROWS
GROUP = 8
PIECE = 40
WIDE = 2 * PIECE
VMEM = pl.BlockSpec(memory_space=pltpu.VMEM)
SMEM = pl.BlockSpec(memory_space=pltpu.SMEM)
HBM = pl.BlockSpec(memory_space=pl.ANY)


def arr(*shape):
    return jax.ShapeDtypeStruct(shape, F32)


def even_place():
    return lax.axis_index("space") % 2 == 0


def put_sends(first, last, near, far):
    even = even_place()

    @pl.when(even)
    def _():
        last(near)
        first(far)

    @pl.when(jnp.logical_not(even))
    def _():
        first(near)
        last(far)


def put_halo(buf, near, far, count, start):
    even = even_place()

    def put(src, row):
        for c in range(C):
            buf[c, row : row + count, :] = src[start + c * count : start + (c + 1) * count, :]

    @pl.when(even)
    def _():
        put(far, BASE - count)
        put(near, BASE + OWN)

    @pl.when(jnp.logical_not(even))
    def _():
        put(near, BASE - count)
        put(far, BASE + OWN)


def pack(src, row, count, start):
    def into(dst):
        for c in range(C):
            dst[start + c * count : start + (c + 1) * count, :] = src[c, row : row + count, :]

    return into


def take_guess(raw, own):
    for c in range(C):
        own[c] = raw[pl.ds(c * OWN * SLICES, OWN, stride=SLICES), :]


def take_forcing(raw, force):
    for c in range(C):
        for r in range(ROWS):
            force[c, pl.ds(r, PLANES, stride=ROWS), :] = raw[c, :, 128 * r : 128 * r + 128] * 0.1


def prep_kernel(guess, forcing, near, far, own, force, raw, fraw, sems):
    one = pltpu.make_async_copy(forcing, fraw, sems.at[0])
    two = pltpu.make_async_copy(guess, raw, sems.at[1])
    one.start()
    two.start()
    one.wait()
    take_forcing(fraw, force)
    two.wait()
    take_guess(raw, own)

    def first(dst):
        pack(own, 0, HALO, 0)(dst)
        pack(force, 0, THREE, C * HALO)(dst)

    def last(dst):
        pack(own, OWN - HALO, HALO, 0)(dst)
        pack(force, OWN - THREE, THREE, C * HALO)(dst)

    put_sends(first, last, near, far)


def gain_kernel(raw, gain_out):
    for c in range(C):
        for r in range(ROWS):
            gain_out[pl.ds(c * OWN + r, PLANES, stride=ROWS), :] = raw[c, :, 128 * r : 128 * r + 128]
    gain_out[C * OWN :, :] = jnp.zeros((gain_out.shape[0] - C * OWN, 128), F32)


def setup_kernel(forcing, lv, cd, st, kl, force, kv, wup, wfix, mask):
    take_forcing(forcing, force)
    lane = lax.broadcasted_iota(jnp.int32, (8, 128), 1)
    row = lax.broadcasted_iota(jnp.int32, (8, 128), 0)
    z = lane % NZ
    edge_row = row % ROWS
    for j in range(C):
        col = [lv[cd[i, j]] for i in range(C)]
        total = functools.reduce(lambda x, y: x + y, col)
        speed = st[kl[j]]
        for i in range(C):
            v = (col[i] - total) + (1.0 - 0.48) - speed if i == j else col[i]
            kv[i * C + j] = jnp.full((8, 128), v, F32)
        wup[j] = jnp.where(z < NZ - 1, 0.08 + speed, 0.0)
    wfix[0] = jnp.where(z > 0, F32(0.08), F32(0.0))
    wfix[1] = jnp.where(jnp.logical_and(lane >= 96, edge_row == ROWS - 1), F32(0.0), F32(0.08))
    wfix[2] = jnp.where(jnp.logical_and(lane < 32, edge_row == 0), F32(0.0), F32(0.08))
    start = lax.axis_index("space") * PLANES - 5
    for t in range(WIN // 8):
        plane = start + 2 * t + row // ROWS
        inside = jnp.logical_and(plane >= 0, plane < NX)
        mask[t] = jnp.where(inside, F32(1.0), F32(0.0))


def clear_edges(buf):
    z = jnp.zeros((C, 8, 128), F32)
    buf[:, 0:8, :] = z
    buf[:, WIN - 8 : WIN, :] = z


def block_step(src, dst, fwin, t, kv, wup, wfix, mask):
    lane = lax.broadcasted_iota(jnp.int32, (8, 128), 1)
    row = lax.broadcasted_iota(jnp.int32, (8, 128), 0)
    low = row < ROWS
    right = lane >= 96
    left = lane < 32
    wdn, wah, wbe = wfix[0], wfix[1], wfix[2]

    def rows(k):
        return pl.ds((t + k) * 8, 8)

    acc = []
    for i in range(C):
        p = [src[i, rows(k), :] for k in (-1, 0, 1, 2)]
        q = [pltpu.roll(v, 4, 0) for v in p]
        pair = []
        for k in (0, 1):
            c = p[k + 1]
            xs = q[k + 1] + jnp.where(low, q[k], q[k + 2])
            up = pltpu.roll(c, 127, 1)
            dn = pltpu.roll(c, 1, 1)
            ra = pltpu.roll(c, 96, 1)
            rb = pltpu.roll(c, 32, 1)
            ah = jnp.where(right, pltpu.roll(ra, 7, 0), ra)
            be = jnp.where(left, pltpu.roll(rb, 1, 0), rb)
            new = fwin[i, rows(k), :] + 0.08 * xs
            new = new + wup[i] * up
            new = new + wdn * dn
            new = new + wah * ah
            new = new + wbe * be
            pair.append(new)
        acc.append(pair)
    for j in range(C):
        c = [src[j, rows(k), :] for k in (0, 1)]
        for i in range(C):
            w = kv[i * C + j]
            acc[i] = [acc[i][k] + w * c[k] for k in (0, 1)]
    for k in (0, 1):
        m = mask[t + k]
        for i in range(C):
            dst[i, rows(k), :] = acc[i][k] * m


def steps(bufs, fwin, plan, coefs):
    for s, (first, count) in enumerate(plan):
        src, dst = bufs[s % 2], bufs[(s + 1) % 2]
        for b in range(count):
            block_step(src, dst, fwin, first + 2 * b, *coefs)


FOUR = ((1, 3), (1, 3), (2, 2), (2, 2))


def first_kernel(guess, force, far, near, kv, wup, wfix, mask, own, state, send_near, send_far, fwin, a, b):
    clear_edges(a)
    clear_edges(b)
    clear_edges(fwin)
    take_guess(guess, own)
    a[:, BASE : BASE + OWN, :] = own[...]
    fwin[:, BASE : BASE + OWN, :] = force[...]
    put_halo(a, near, far, HALO, 0)
    put_halo(fwin, near, far, THREE, C * HALO)
    steps((a, b), fwin, FOUR, (kv, wup, wfix, mask))
    state[...] = a[:, BASE : BASE + OWN, :]
    put_sends(pack(state, 0, HALO, 0), pack(state, OWN - HALO, HALO, 0), send_near, send_far)


def second_kernel(state, far, near, fwin, gain, kv, wup, wfix, mask, out, a, b):
    clear_edges(a)
    clear_edges(b)
    a[:, BASE : BASE + OWN, :] = state[...]
    put_halo(a, near, far, HALO, 0)
    steps((a, b), fwin, FOUR, (kv, wup, wfix, mask))
    use = jnp.where(lax.axis_index("tm") > 0, F32(1.0), F32(0.0))
    tiles = OWN // 8
    for t in range(GROUP * PIECE // 8):
        p, r = divmod(t, PIECE // 8)
        here = pl.ds(p * WIDE + r * 8, 8)
        there = pl.ds(p * WIDE + PIECE + r * 8, 8)
        if t < C * tiles:
            c, x = divmod(t, tiles)
            u = state[c, x * 8 : x * 8 + 8, :]
            v = a[c, BASE + x * 8 : BASE + x * 8 + 8, :]
            out[here, :] = v - use * (gain[t * 8 : t * 8 + 8, :] * u)
            out[there, :] = u
        else:
            out[here, :] = jnp.zeros((8, 128), F32)
            out[there, :] = jnp.zeros((8, 128), F32)


def my_gain(gain):
    place = GROUP - 1 - lax.axis_index("tm") % GROUP
    return gain[pl.ds(pl.multiple_of(place * PIECE, 8), PIECE), :]


def slot(i, width=PIECE, half=0):
    start = (GROUP - 1 - i) * width + half * PIECE
    return slice(start, start + PIECE)


def local_kernel(pieces, gain, sums, total, tail):
    mine = my_gain(gain)
    running = pieces[slot(0, WIDE), :]
    sums[slot(0), :] = running
    for i in range(1, GROUP):
        running = mine * running + pieces[slot(i, WIDE), :]
        sums[slot(i), :] = running
        if i == GROUP - 2:
            tail[:PIECE, :] = running
    tail[PIECE:, :] = pieces[slot(GROUP - 1, WIDE, 1), :]
    for i in range(GROUP):
        total[slot(i), :] = running


def prefix_kernel(totals, tail, sums, pieces, gain, out):
    group = lax.axis_index("tm") // GROUP
    g1 = my_gain(gain)
    g2 = g1 * g1
    g4 = g2 * g2
    g8 = g4 * g4
    before = jnp.zeros((PIECE, 128), F32)
    ahead = before
    for g in range(GROUP - 1):
        take = g < group
        ahead = jnp.where(take, before, ahead)
        before = jnp.where(take, g8 * before + totals[slot(g), :], before)
    for i in range(GROUP):
        if i == 0:
            base = tail[PIECE:, :]
            value = tail[:PIECE, :] + (g4 * g2 * g1) * ahead
        else:
            base = pieces[slot(i - 1, WIDE, 1), :]
            if i == 1:
                value = jnp.where(group > 0, before, base)
            else:
                before = g1 * before
                value = sums[slot(i - 2), :] + before
        out[slot(i, WIDE), :] = value
        out[slot(i, WIDE, 1), :] = value - base


def gather_kernel(pieces, own, state, near, far):
    first = lax.axis_index("tm") == 0

    @pl.when(first)
    def _():
        state[...] = own[...]

    @pl.when(jnp.logical_not(first))
    def _():
        tiles = OWN // 8
        for t in range(C * tiles):
            c, x = divmod(t, tiles)
            p, r = divmod(t, PIECE // 8)
            state[c, x * 8 : x * 8 + 8, :] = pieces[p * WIDE + r * 8 : p * WIDE + r * 8 + 8, :]

    put_sends(pack(state, 0, THREE, 0), pack(state, OWN - THREE, THREE, 0), near, far)


def last_kernel(state, far, near, fwin, pieces, kv, wup, wfix, mask, out, corr, a, b):
    clear_edges(a)
    clear_edges(b)
    a[:, BASE : BASE + OWN, :] = state[...]
    put_halo(a, near, far, THREE, 0)

    def emit(buf, j):
        for c in range(C):
            out[pl.ds(c * OWN * SLICES + j, OWN, stride=SLICES), :] = buf[c, BASE : BASE + OWN, :]

    emit(a, 0)
    bufs = (a, b)
    for j, one in enumerate(((1, 3), (2, 2), (2, 2))):
        src, dst = bufs[j % 2], bufs[(j + 1) % 2]
        steps((src, dst), fwin, (one,), (kv, wup, wfix, mask))
        emit(dst, j + 1)
    late = lax.axis_index("tm") >= 1
    for t in range(C * OWN // 8):
        p, r = divmod(t, PIECE // 8)
        start = p * WIDE + PIECE + r * 8
        corr[t * 8 : t * 8 + 8, :] = jnp.where(late, pieces[start : start + 8, :], 0.0)


WORK = [pltpu.VMEM((C, WIN, 128), F32), pltpu.VMEM((C, WIN, 128), F32)]


def call(kernel, ins, outs, scratch=(), place=None, grant=32):
    return pl.pallas_call(
        kernel,
        out_shape=outs,
        in_specs=place or [VMEM] * len(ins),
        out_specs=[VMEM] * len(outs),
        scratch_shapes=list(scratch),
        compiler_params=pltpu.CompilerParams(vmem_limit_bytes=grant * 1024 * 1024),
        name=kernel.__name__,
    )(*ins)


def exchange(near, far):
    places = lax.axis_size("space")
    inner = [(i, i ^ 1) for i in range(places)]
    outer = [(i, j) for i in range(places) for j in [i - 1 if i % 2 == 0 else i + 1] if 0 <= j < places]
    far = lax.ppermute(far, "space", outer)
    near = lax.ppermute(near, "space", inner)
    return near, far


def swap(value, stride):
    count = lax.axis_size("tm")
    firsts = [i for i in range(count) if (i // stride) % GROUP == 0]
    groups = [[i + stride * j for j in reversed(range(GROUP))] for i in firsts]
    slots = value.reshape(GROUP, -1, 128)
    return lax.all_to_all(slots, "tm", 0, 0, tiled=True, axis_index_groups=groups).reshape(value.shape)


def shards(guess, forcing, coarse_gain, kernel_levels, kernel_code, settle_levels, settle_class):
    intervals = lax.axis_size("tm")
    rows = guess.reshape(SLICES, C, PLANES, ROWS, 128).transpose(1, 2, 3, 0, 4).reshape(C * OWN * SLICES, 128)
    slab = arr(C, OWN, 128)
    wide, four, three = (arr(C * n, 128) for n in (HALO + THREE, HALO, THREE))
    pieces, double = arr(GROUP * PIECE, 128), arr(GROUP * WIDE, 128)
    near, far = call(
        prep_kernel,
        [rows, forcing],
        [wide, wide],
        [pltpu.VMEM(slab.shape, F32), pltpu.VMEM(slab.shape, F32), pltpu.VMEM(rows.shape, F32), pltpu.VMEM(forcing.shape, F32), pltpu.SemaphoreType.DMA((2,))],
        [HBM] * 2,
        60,
    )
    near, far = exchange(near, far)
    small = (kernel_levels, kernel_code, settle_levels, settle_class)
    force, *coefs = call(
        setup_kernel,
        [forcing, *small],
        [slab, arr(C * C, 8, 128), arr(C, 8, 128), arr(3, 8, 128), arr(WIN // 8, 8, 128)],
        place=[VMEM] + [SMEM] * len(small),
    )
    (gain,) = call(gain_kernel, [coarse_gain], [pieces])
    own, state, near, far, fwin = call(
        first_kernel,
        [rows, force, far, near, *coefs],
        [slab, slab, four, four, arr(C, WIN, 128)],
        WORK,
    )
    near, far = exchange(near, far)
    (element,) = call(second_kernel, [state, far, near, fwin, gain, *coefs], [double], WORK)
    spread = swap(element, 1)
    sums, totals, tail = call(local_kernel, [spread, gain], [pieces, pieces, arr(WIDE, 128)])
    totals = swap(totals, GROUP)
    tail = lax.ppermute(tail, "tm", [(i, i + GROUP) for i in range(intervals - GROUP)])
    (back,) = call(prefix_kernel, [totals, tail, sums, spread, gain], [double])
    back = swap(back, 1)
    state, near, far = call(
        gather_kernel, [back, own], [slab, three, three]
    )
    near, far = exchange(near, far)
    updated, corr = call(
        last_kernel,
        [state, far, near, fwin, back, *coefs],
        [arr(C * OWN * SLICES, 128), arr(C * OWN, 128)],
        WORK,
    )
    updated = updated.reshape(C, PLANES, ROWS, SLICES, 128).transpose(3, 0, 1, 2, 4)
    return (
        updated.reshape(SLICES, C, PLANES, ROWS * 128),
        corr.reshape(1, C, PLANES, ROWS * 128),
    )


def solution(mesh):
    in_specs = (
        P("tm", None, "space", None),
        P(None, "space", None),
        P(None, "space", None),
        P(),
        P(),
        P(),
        P(),
    )
    out_specs = (P("tm", None, "space", None), P("tm", None, "space", None))
    return jax.shard_map(shards, mesh=mesh, in_specs=in_specs, out_specs=out_specs, check_vma=False)
```

```python
import functools

import jax
import jax.numpy as jnp
from jax import lax
from jax.experimental import pallas as pl
from jax.experimental.pallas import tpu as pltpu
from jax.sharding import PartitionSpec as P

F32 = jnp.float32
C = 12
NY = 16
NZ = 32
PLANES = 6
NX = 48
SLICES = 4
ROWS = 4
OWN = PLANES * ROWS
HALO = 4 * ROWS
THREE = 3 * ROWS
WIN = 64
BASE = 5 * ROWS
GROUP = 8
PIECE = C * OWN // GROUP
WIDE = 2 * PIECE
SPACED = 40
CHUNK = 12
VMEM = pl.BlockSpec(memory_space=pltpu.VMEM)
SMEM = pl.BlockSpec(memory_space=pltpu.SMEM)
HBM = pl.BlockSpec(memory_space=pl.ANY)


def arr(*shape):
    return jax.ShapeDtypeStruct(shape, F32)


def even_place():
    return lax.axis_index("space") % 2 == 0


def put_sends(first, last, near, far):
    even = even_place()

    @pl.when(even)
    def _():
        last(near)
        first(far)

    @pl.when(jnp.logical_not(even))
    def _():
        first(near)
        last(far)


def put_halo(buf, near, far, count, start):
    even = even_place()

    def put(src, row):
        for c in range(C):
            buf[c, row : row + count, :] = src[start + c * count : start + (c + 1) * count, :]

    @pl.when(even)
    def _():
        put(far, BASE - count)
        put(near, BASE + OWN)

    @pl.when(jnp.logical_not(even))
    def _():
        put(near, BASE - count)
        put(far, BASE + OWN)


def pack(src, row, count, start):
    def into(dst):
        for c in range(C):
            dst[start + c * count : start + (c + 1) * count, :] = src[c, row : row + count, :]

    return into


def take_guess(raw, own):
    for c in range(C):
        own[c] = raw[pl.ds(c * OWN * SLICES, OWN, stride=SLICES), :]


def take_forcing(raw, force):
    for c in range(C):
        for r in range(ROWS):
            force[c, pl.ds(r, PLANES, stride=ROWS), :] = raw[c, :, 128 * r : 128 * r + 128] * 0.1


def prep_kernel(guess, forcing, own, force, near, far, raw, fraw, sems):
    one = pltpu.make_async_copy(forcing, fraw, sems.at[0])
    two = pltpu.make_async_copy(guess, raw, sems.at[1])
    one.start()
    two.start()
    one.wait()
    take_forcing(fraw, force)
    two.wait()
    take_guess(raw, own)

    def first(dst):
        pack(own, 0, HALO, 0)(dst)
        pack(force, 0, THREE, C * HALO)(dst)

    def last(dst):
        pack(own, OWN - HALO, HALO, 0)(dst)
        pack(force, OWN - THREE, THREE, C * HALO)(dst)

    put_sends(first, last, near, far)


def gain_kernel(raw, rows, spaced):
    for c in range(C):
        for r in range(ROWS):
            rows[pl.ds(c * OWN + r, PLANES, stride=ROWS), :] = raw[c, :, 128 * r : 128 * r + 128]
    for p in range(GROUP):
        spaced[p * SPACED : p * SPACED + PIECE, :] = rows[p * PIECE : (p + 1) * PIECE, :]


def setup_kernel(lv, cd, st, kl, kv, wup, wfix, mask):
    lane = lax.broadcasted_iota(jnp.int32, (8, 128), 1)
    row = lax.broadcasted_iota(jnp.int32, (8, 128), 0)
    z = lane % NZ
    edge_row = row % ROWS
    for j in range(C):
        col = [lv[cd[i, j]] for i in range(C)]
        total = functools.reduce(lambda x, y: x + y, col)
        speed = st[kl[j]]
        for i in range(C):
            v = (col[i] - total) + (1.0 - 0.48) - speed if i == j else col[i]
            kv[i * C + j] = jnp.full((8, 128), v, F32)
        wup[j] = jnp.where(z < NZ - 1, 0.08 + speed, 0.0)
    wfix[0] = jnp.where(z > 0, F32(0.08), F32(0.0))
    wfix[1] = jnp.where(jnp.logical_and(lane >= 96, edge_row == ROWS - 1), F32(0.0), F32(0.08))
    wfix[2] = jnp.where(jnp.logical_and(lane < 32, edge_row == 0), F32(0.0), F32(0.08))
    start = lax.axis_index("space") * PLANES - 5
    for t in range(WIN // 8):
        plane = start + 2 * t + row // ROWS
        inside = jnp.logical_and(plane >= 0, plane < NX)
        mask[t] = jnp.where(inside, F32(1.0), F32(0.0))


def clear_edges(buf):
    z = jnp.zeros((C, 8, 128), F32)
    buf[:, 0:8, :] = z
    buf[:, WIN - 8 : WIN, :] = z


def block_step(src, dst, fwin, t, kv, wup, wfix, mask):
    lane = lax.broadcasted_iota(jnp.int32, (8, 128), 1)
    row = lax.broadcasted_iota(jnp.int32, (8, 128), 0)
    low = row < ROWS
    right = lane >= 96
    left = lane < 32
    wdn, wah, wbe = wfix[0], wfix[1], wfix[2]

    def rows(k):
        return pl.ds((t + k) * 8, 8)

    acc = []
    for i in range(C):
        p = [src[i, rows(k), :] for k in (-1, 0, 1, 2)]
        q = [pltpu.roll(v, 4, 0) for v in p]
        pair = []
        for k in (0, 1):
            c = p[k + 1]
            xs = q[k + 1] + jnp.where(low, q[k], q[k + 2])
            up = pltpu.roll(c, 127, 1)
            dn = pltpu.roll(c, 1, 1)
            ra = pltpu.roll(c, 96, 1)
            rb = pltpu.roll(c, 32, 1)
            ah = jnp.where(right, pltpu.roll(ra, 7, 0), ra)
            be = jnp.where(left, pltpu.roll(rb, 1, 0), rb)
            new = fwin[i, rows(k), :] + 0.08 * xs
            new = new + wup[i] * up
            new = new + wdn * dn
            new = new + wah * ah
            new = new + wbe * be
            pair.append(new)
        acc.append(pair)
    for j in range(C):
        c = [src[j, rows(k), :] for k in (0, 1)]
        for i in range(C):
            w = kv[i * C + j]
            acc[i] = [acc[i][k] + w * c[k] for k in (0, 1)]
    for k in (0, 1):
        m = mask[t + k]
        for i in range(C):
            dst[i, rows(k), :] = acc[i][k] * m


def steps(bufs, fwin, plan, coefs):
    for s, (first, count) in enumerate(plan):
        src, dst = bufs[s % 2], bufs[(s + 1) % 2]
        for b in range(count):
            block_step(src, dst, fwin, first + 2 * b, *coefs)


FOUR = ((1, 3), (1, 3), (2, 2), (2, 2))


def chunks():
    for t in range(C * OWN // CHUNK):
        c, x = divmod(t * CHUNK, OWN)
        p, r = divmod(t * CHUNK, PIECE)
        yield c, x, p, r


def first_kernel(own, force, far, near, kv, wup, wfix, mask, state, send_near, send_far, fwin, a, b):
    clear_edges(a)
    clear_edges(b)
    clear_edges(fwin)
    a[:, BASE : BASE + OWN, :] = own[...]
    fwin[:, BASE : BASE + OWN, :] = force[...]
    put_halo(a, near, far, HALO, 0)
    put_halo(fwin, near, far, THREE, C * HALO)
    steps((a, b), fwin, FOUR, (kv, wup, wfix, mask))
    state[...] = a[:, BASE : BASE + OWN, :]
    put_sends(pack(state, 0, HALO, 0), pack(state, OWN - HALO, HALO, 0), send_near, send_far)


def second_kernel(state, far, near, fwin, gain, kv, wup, wfix, mask, out, a, b):
    clear_edges(a)
    clear_edges(b)
    a[:, BASE : BASE + OWN, :] = state[...]
    put_halo(a, near, far, HALO, 0)
    steps((a, b), fwin, FOUR, (kv, wup, wfix, mask))
    use = jnp.where(lax.axis_index("tm") > 0, F32(1.0), F32(0.0))
    for c, x, p, r in chunks():
        u = state[c, x : x + CHUNK, :]
        v = a[c, BASE + x : BASE + x + CHUNK, :]
        row = p * WIDE + r
        out[row : row + CHUNK, :] = v - use * (gain[c * OWN + x : c * OWN + x + CHUNK, :] * u)
        out[row + PIECE : row + PIECE + CHUNK, :] = u


def my_gain(gain):
    place = GROUP - 1 - lax.axis_index("tm") % GROUP
    return gain[pl.ds(pl.multiple_of(place * SPACED, 8), PIECE), :]


def slot(i, width=PIECE, half=0):
    start = (GROUP - 1 - i) * width + half * PIECE
    return slice(start, start + PIECE)


def local_kernel(pieces, gain, sums, total, tail):
    mine = my_gain(gain)
    running = pieces[slot(0, WIDE), :]
    sums[slot(0), :] = running
    for i in range(1, GROUP):
        running = mine * running + pieces[slot(i, WIDE), :]
        sums[slot(i), :] = running
        if i == GROUP - 2:
            tail[:PIECE, :] = running
    tail[PIECE:, :] = pieces[slot(GROUP - 1, WIDE, 1), :]
    for i in range(GROUP):
        total[slot(i), :] = running


def prefix_kernel(totals, tail, sums, pieces, gain, out):
    group = lax.axis_index("tm") // GROUP
    g1 = my_gain(gain)
    g2 = g1 * g1
    g4 = g2 * g2
    g8 = g4 * g4
    before = jnp.zeros((PIECE, 128), F32)
    ahead = before
    for g in range(GROUP - 1):
        take = g < group
        ahead = jnp.where(take, before, ahead)
        before = jnp.where(take, g8 * before + totals[slot(g), :], before)
    for i in range(GROUP):
        if i == 0:
            base = tail[PIECE:, :]
            value = tail[:PIECE, :] + (g4 * g2 * g1) * ahead
        else:
            base = pieces[slot(i - 1, WIDE, 1), :]
            if i == 1:
                value = jnp.where(group > 0, before, base)
            else:
                before = g1 * before
                value = sums[slot(i - 2), :] + before
        out[slot(i, WIDE), :] = value
        out[slot(i, WIDE, 1), :] = value - base


def gather_kernel(pieces, own, state, near, far):
    first = lax.axis_index("tm") == 0

    @pl.when(first)
    def _():
        state[...] = own[...]

    @pl.when(jnp.logical_not(first))
    def _():
        for c, x, p, r in chunks():
            state[c, x : x + CHUNK, :] = pieces[p * WIDE + r : p * WIDE + r + CHUNK, :]

    put_sends(pack(state, 0, THREE, 0), pack(state, OWN - THREE, THREE, 0), near, far)


def last_kernel(state, far, near, fwin, pieces, kv, wup, wfix, mask, out, corr, a, b):
    clear_edges(a)
    clear_edges(b)
    a[:, BASE : BASE + OWN, :] = state[...]
    put_halo(a, near, far, THREE, 0)

    def emit(buf, j):
        for c in range(C):
            out[pl.ds(c * OWN * SLICES + j, OWN, stride=SLICES), :] = buf[c, BASE : BASE + OWN, :]

    emit(a, 0)
    bufs = (a, b)
    for j, one in enumerate(((1, 3), (2, 2), (2, 2))):
        src, dst = bufs[j % 2], bufs[(j + 1) % 2]
        steps((src, dst), fwin, (one,), (kv, wup, wfix, mask))
        emit(dst, j + 1)
    late = lax.axis_index("tm") >= 1
    for c, x, p, r in chunks():
        row, start = c * OWN + x, p * WIDE + PIECE + r
        corr[row : row + CHUNK, :] = jnp.where(late, pieces[start : start + CHUNK, :], 0.0)


WORK = [pltpu.VMEM((C, WIN, 128), F32), pltpu.VMEM((C, WIN, 128), F32)]


def call(kernel, ins, outs, scratch=(), place=None, grant=32):
    return pl.pallas_call(
        kernel,
        out_shape=outs,
        in_specs=place or [VMEM] * len(ins),
        out_specs=[VMEM] * len(outs),
        scratch_shapes=list(scratch),
        compiler_params=pltpu.CompilerParams(vmem_limit_bytes=int(grant * 1024 * 1024)),
        name=kernel.__name__,
    )(*ins)


def exchange(near, far):
    places = lax.axis_size("space")
    inner = [(i, i ^ 1) for i in range(places)]
    outer = [(i, j) for i in range(places) for j in [i - 1 if i % 2 == 0 else i + 1] if 0 <= j < places]
    far = lax.ppermute(far, "space", outer)
    near = lax.ppermute(near, "space", inner)
    return near, far


def swap(value, stride):
    count = lax.axis_size("tm")
    firsts = [i for i in range(count) if (i // stride) % GROUP == 0]
    groups = [[i + stride * j for j in reversed(range(GROUP))] for i in firsts]
    slots = value.reshape(GROUP, -1)
    return lax.all_to_all(slots, "tm", 0, 0, tiled=True, axis_index_groups=groups).reshape(value.shape)


def shards(guess, forcing, coarse_gain, kernel_levels, kernel_code, settle_levels, settle_class):
    intervals = lax.axis_size("tm")
    rows = guess.reshape(SLICES, C, PLANES, ROWS, 128).transpose(1, 2, 3, 0, 4).reshape(C * OWN * SLICES, 128)
    slab = arr(C, OWN, 128)
    wide, four, three = (arr(C * n, 128) for n in (HALO + THREE, HALO, THREE))
    pieces, double = arr(GROUP * PIECE, 128), arr(GROUP * WIDE, 128)
    own, force, near, far = call(
        prep_kernel,
        [rows, forcing],
        [slab, slab, wide, wide],
        [pltpu.VMEM(rows.shape, F32), pltpu.VMEM(forcing.shape, F32), pltpu.SemaphoreType.DMA((2,))],
        [HBM] * 2,
        53.25,
    )
    near, far = exchange(near, far)
    small = (kernel_levels, kernel_code, settle_levels, settle_class)
    coefs = call(
        setup_kernel,
        list(small),
        [arr(C * C, 8, 128), arr(C, 8, 128), arr(3, 8, 128), arr(WIN // 8, 8, 128)],
        place=[SMEM] * len(small),
    )
    gain, spaced = call(gain_kernel, [coarse_gain], [pieces, arr(GROUP * SPACED, 128)])
    state, near, far, fwin = call(
        first_kernel,
        [own, force, far, near, *coefs],
        [slab, four, four, arr(C, WIN, 128)],
        WORK,
    )
    near, far = exchange(near, far)
    (element,) = call(second_kernel, [state, far, near, fwin, gain, *coefs], [double], WORK)
    spread = swap(element, 1)
    sums, totals, tail = call(local_kernel, [spread, spaced], [pieces, pieces, arr(WIDE, 128)])
    totals = swap(totals, GROUP)
    tail = lax.ppermute(tail, "tm", [(i, i + GROUP) for i in range(intervals - GROUP)])
    (back,) = call(prefix_kernel, [totals, tail, sums, spread, spaced], [double])
    back = swap(back, 1)
    state, near, far = call(
        gather_kernel, [back, own], [slab, three, three]
    )
    near, far = exchange(near, far)
    updated, corr = call(
        last_kernel,
        [state, far, near, fwin, back, *coefs],
        [arr(C * OWN * SLICES, 128), arr(C * OWN, 128)],
        WORK,
    )
    updated = updated.reshape(C, PLANES, ROWS, SLICES, 128).transpose(3, 0, 1, 2, 4)
    return (
        updated.reshape(SLICES, C, PLANES, ROWS * 128),
        corr.reshape(1, C, PLANES, ROWS * 128),
    )


def solution(mesh):
    in_specs = (
        P("tm", None, "space", None),
        P(None, "space", None),
        P(None, "space", None),
        P(),
        P(),
        P(),
        P(),
    )
    out_specs = (P("tm", None, "space", None), P("tm", None, "space", None))
    return jax.shard_map(shards, mesh=mesh, in_specs=in_specs, out_specs=out_specs, check_vma=False)
```

```python
import functools

import jax
import jax.numpy as jnp
from jax import lax
from jax.experimental import pallas as pl
from jax.experimental.pallas import tpu as pltpu
from jax.sharding import PartitionSpec as P

F32 = jnp.float32
C = 12
NY = 16
NZ = 32
PLANES = 6
NX = 48
SLICES = 4
ROWS = 4
OWN = PLANES * ROWS
HALO = 4 * ROWS
THREE = 3 * ROWS
WIN = 64
BASE = 5 * ROWS
GROUP = 8
DOWN = (7, 6, 5, 4, 3, 2, 1, 0)
MIDDLE = (4, 7, 6, 5, 3, 2, 1, 0)
PIECE = C * OWN // GROUP
WIDE = 2 * PIECE
SPACED = 40
CHUNK = 12
VMEM = pl.BlockSpec(memory_space=pltpu.VMEM)
SMEM = pl.BlockSpec(memory_space=pltpu.SMEM)
HBM = pl.BlockSpec(memory_space=pl.ANY)


def arr(*shape):
    return jax.ShapeDtypeStruct(shape, F32)


def even_place():
    return lax.axis_index("space") % 2 == 0


def put_sends(first, last, near, far):
    even = even_place()

    @pl.when(even)
    def _():
        last(near)
        first(far)

    @pl.when(jnp.logical_not(even))
    def _():
        first(near)
        last(far)


def put_halo(buf, near, far, count, start):
    even = even_place()

    def put(src, row):
        for c in range(C):
            buf[c, row : row + count, :] = src[start + c * count : start + (c + 1) * count, :]

    @pl.when(even)
    def _():
        put(far, BASE - count)
        put(near, BASE + OWN)

    @pl.when(jnp.logical_not(even))
    def _():
        put(near, BASE - count)
        put(far, BASE + OWN)


def pack(src, row, count, start):
    def into(dst):
        for c in range(C):
            dst[start + c * count : start + (c + 1) * count, :] = src[c, row : row + count, :]

    return into


def take_guess(raw, own):
    for c in range(C):
        own[c] = raw[pl.ds(c * OWN * SLICES, OWN, stride=SLICES), :]


def take_forcing(raw, force):
    for c in range(C):
        for r in range(ROWS):
            force[c, pl.ds(r, PLANES, stride=ROWS), :] = raw[c, :, 128 * r : 128 * r + 128] * 0.1


def prep_kernel(guess, forcing, own, force, near, far, raw, fraw, sems):
    one = pltpu.make_async_copy(forcing, fraw, sems.at[0])
    two = pltpu.make_async_copy(guess, raw, sems.at[1])
    one.start()
    two.start()
    one.wait()
    take_forcing(fraw, force)
    two.wait()
    take_guess(raw, own)

    def first(dst):
        pack(own, 0, HALO, 0)(dst)
        pack(force, 0, THREE, C * HALO)(dst)

    def last(dst):
        pack(own, OWN - HALO, HALO, 0)(dst)
        pack(force, OWN - THREE, THREE, C * HALO)(dst)

    put_sends(first, last, near, far)


def gain_kernel(raw, rows, spaced):
    for c in range(C):
        for r in range(ROWS):
            rows[pl.ds(c * OWN + r, PLANES, stride=ROWS), :] = raw[c, :, 128 * r : 128 * r + 128]
    for p in range(GROUP):
        spaced[p * SPACED : p * SPACED + PIECE, :] = rows[p * PIECE : (p + 1) * PIECE, :]


def setup_kernel(lv, cd, st, kl, kv, wup, wfix, mask):
    lane = lax.broadcasted_iota(jnp.int32, (8, 128), 1)
    row = lax.broadcasted_iota(jnp.int32, (8, 128), 0)
    z = lane % NZ
    edge_row = row % ROWS
    for j in range(C):
        col = [lv[cd[i, j]] for i in range(C)]
        total = functools.reduce(lambda x, y: x + y, col)
        speed = st[kl[j]]
        for i in range(C):
            v = (col[i] - total) + (1.0 - 0.48) - speed if i == j else col[i]
            kv[i * C + j] = jnp.full((8, 128), v, F32)
        wup[j] = jnp.where(z < NZ - 1, 0.08 + speed, 0.0)
    wfix[0] = jnp.where(z > 0, F32(0.08), F32(0.0))
    wfix[1] = jnp.where(jnp.logical_and(lane >= 96, edge_row == ROWS - 1), F32(0.0), F32(0.08))
    wfix[2] = jnp.where(jnp.logical_and(lane < 32, edge_row == 0), F32(0.0), F32(0.08))
    start = lax.axis_index("space") * PLANES - 5
    for t in range(WIN // 8):
        plane = start + 2 * t + row // ROWS
        inside = jnp.logical_and(plane >= 0, plane < NX)
        mask[t] = jnp.where(inside, F32(1.0), F32(0.0))


def clear_edges(buf):
    z = jnp.zeros((C, 8, 128), F32)
    buf[:, 0:8, :] = z
    buf[:, WIN - 8 : WIN, :] = z


def block_step(src, dst, fwin, t, kv, wup, wfix, mask):
    lane = lax.broadcasted_iota(jnp.int32, (8, 128), 1)
    row = lax.broadcasted_iota(jnp.int32, (8, 128), 0)
    low = row < ROWS
    right = lane >= 96
    left = lane < 32
    wdn, wah, wbe = wfix[0], wfix[1], wfix[2]

    def rows(k):
        return pl.ds((t + k) * 8, 8)

    acc = []
    for i in range(C):
        p = [src[i, rows(k), :] for k in (-1, 0, 1, 2)]
        q = [pltpu.roll(v, 4, 0) for v in p]
        pair = []
        for k in (0, 1):
            c = p[k + 1]
            xs = q[k + 1] + jnp.where(low, q[k], q[k + 2])
            up = pltpu.roll(c, 127, 1)
            dn = pltpu.roll(c, 1, 1)
            ra = pltpu.roll(c, 96, 1)
            rb = pltpu.roll(c, 32, 1)
            ah = jnp.where(right, pltpu.roll(ra, 7, 0), ra)
            be = jnp.where(left, pltpu.roll(rb, 1, 0), rb)
            new = fwin[i, rows(k), :] + 0.08 * xs
            new = new + wup[i] * up
            new = new + wdn * dn
            new = new + wah * ah
            new = new + wbe * be
            pair.append(new)
        acc.append(pair)
    for j in range(C):
        c = [src[j, rows(k), :] for k in (0, 1)]
        for i in range(C):
            w = kv[i * C + j]
            acc[i] = [acc[i][k] + w * c[k] for k in (0, 1)]
    for k in (0, 1):
        m = mask[t + k]
        for i in range(C):
            dst[i, rows(k), :] = acc[i][k] * m


def steps(bufs, fwin, plan, coefs):
    for s, (first, count) in enumerate(plan):
        src, dst = bufs[s % 2], bufs[(s + 1) % 2]
        for b in range(count):
            block_step(src, dst, fwin, first + 2 * b, *coefs)


FOUR = ((1, 3), (1, 3), (2, 2), (2, 2))


def chunks():
    for t in range(C * OWN // CHUNK):
        c, x = divmod(t * CHUNK, OWN)
        p, r = divmod(t * CHUNK, PIECE)
        yield c, x, p, r


def first_kernel(own, force, far, near, kv, wup, wfix, mask, state, send_near, send_far, fwin, a, b):
    clear_edges(a)
    clear_edges(b)
    clear_edges(fwin)
    a[:, BASE : BASE + OWN, :] = own[...]
    fwin[:, BASE : BASE + OWN, :] = force[...]
    put_halo(a, near, far, HALO, 0)
    put_halo(fwin, near, far, THREE, C * HALO)
    steps((a, b), fwin, FOUR, (kv, wup, wfix, mask))
    state[...] = a[:, BASE : BASE + OWN, :]
    put_sends(pack(state, 0, HALO, 0), pack(state, OWN - HALO, HALO, 0), send_near, send_far)


def second_kernel(state, far, near, fwin, gain, kv, wup, wfix, mask, out, a, b):
    clear_edges(a)
    clear_edges(b)
    a[:, BASE : BASE + OWN, :] = state[...]
    put_halo(a, near, far, HALO, 0)
    steps((a, b), fwin, FOUR, (kv, wup, wfix, mask))
    use = jnp.where(lax.axis_index("tm") > 0, F32(1.0), F32(0.0))
    for c, x, p, r in chunks():
        u = state[c, x : x + CHUNK, :]
        v = a[c, BASE + x : BASE + x + CHUNK, :]
        row = p * WIDE + r
        out[row : row + CHUNK, :] = v - use * (gain[c * OWN + x : c * OWN + x + CHUNK, :] * u)
        out[row + PIECE : row + PIECE + CHUNK, :] = u


def my_gain(gain):
    place = GROUP - 1 - lax.axis_index("tm") % GROUP
    return gain[pl.ds(pl.multiple_of(place * SPACED, 8), PIECE), :]


def slot(i, width=PIECE, half=0):
    start = (GROUP - 1 - i) * width + half * PIECE
    return slice(start, start + PIECE)


def local_kernel(pieces, gain, sums, total, tail):
    mine = my_gain(gain)
    running = pieces[slot(0, WIDE), :]
    sums[slot(0), :] = running
    for i in range(1, GROUP):
        running = mine * running + pieces[slot(i, WIDE), :]
        sums[slot(i), :] = running
        if i == GROUP - 2:
            tail[:PIECE, :] = running
    tail[PIECE:, :] = pieces[slot(GROUP - 1, WIDE, 1), :]
    for i in range(GROUP):
        total[i * PIECE : (i + 1) * PIECE, :] = running


def prefix_kernel(totals, tail, sums, pieces, gain, out):
    group = lax.axis_index("tm") // GROUP
    g1 = my_gain(gain)
    g2 = g1 * g1
    g4 = g2 * g2
    g8 = g4 * g4
    before = jnp.zeros((PIECE, 128), F32)
    ahead = before
    for g in range(GROUP - 1):
        take = g < group
        ahead = jnp.where(take, before, ahead)
        start = MIDDLE.index(g) * PIECE
        before = jnp.where(take, g8 * before + totals[start : start + PIECE, :], before)
    for i in range(GROUP):
        if i == 0:
            base = tail[PIECE:, :]
            value = tail[:PIECE, :] + (g4 * g2 * g1) * ahead
        else:
            base = pieces[slot(i - 1, WIDE, 1), :]
            if i == 1:
                value = jnp.where(group > 0, before, base)
            else:
                before = g1 * before
                value = sums[slot(i - 2), :] + before
        out[slot(i, WIDE), :] = value
        out[slot(i, WIDE, 1), :] = value - base


def gather_kernel(pieces, own, state, near, far):
    first = lax.axis_index("tm") == 0

    @pl.when(first)
    def _():
        state[...] = own[...]

    @pl.when(jnp.logical_not(first))
    def _():
        for c, x, p, r in chunks():
            state[c, x : x + CHUNK, :] = pieces[p * WIDE + r : p * WIDE + r + CHUNK, :]

    put_sends(pack(state, 0, THREE, 0), pack(state, OWN - THREE, THREE, 0), near, far)


def last_kernel(state, far, near, fwin, pieces, kv, wup, wfix, mask, out, corr, a, b):
    clear_edges(a)
    clear_edges(b)
    a[:, BASE : BASE + OWN, :] = state[...]
    put_halo(a, near, far, THREE, 0)

    def emit(buf, j):
        for c in range(C):
            out[pl.ds(c * OWN * SLICES + j, OWN, stride=SLICES), :] = buf[c, BASE : BASE + OWN, :]

    emit(a, 0)
    bufs = (a, b)
    for j, one in enumerate(((1, 3), (2, 2), (2, 2))):
        src, dst = bufs[j % 2], bufs[(j + 1) % 2]
        steps((src, dst), fwin, (one,), (kv, wup, wfix, mask))
        emit(dst, j + 1)
    late = lax.axis_index("tm") >= 1
    for c, x, p, r in chunks():
        row, start = c * OWN + x, p * WIDE + PIECE + r
        corr[row : row + CHUNK, :] = jnp.where(late, pieces[start : start + CHUNK, :], 0.0)


WORK = [pltpu.VMEM((C, WIN, 128), F32), pltpu.VMEM((C, WIN, 128), F32)]


def call(kernel, ins, outs, scratch=(), place=None, grant=32):
    return pl.pallas_call(
        kernel,
        out_shape=outs,
        in_specs=place or [VMEM] * len(ins),
        out_specs=[VMEM] * len(outs),
        scratch_shapes=list(scratch),
        compiler_params=pltpu.CompilerParams(vmem_limit_bytes=int(grant * 1024 * 1024)),
        name=kernel.__name__,
    )(*ins)


def exchange(near, far):
    places = lax.axis_size("space")
    inner = [(i, i ^ 1) for i in range(places)]
    outer = [(i, j) for i in range(places) for j in [i - 1 if i % 2 == 0 else i + 1] if 0 <= j < places]
    far = lax.ppermute(far, "space", outer)
    near = lax.ppermute(near, "space", inner)
    return near, far


def swap(value, stride, order):
    count = lax.axis_size("tm")
    firsts = [i for i in range(count) if (i // stride) % GROUP == 0]
    groups = [[i + stride * j for j in order] for i in firsts]
    slots = value.reshape(GROUP, -1)
    return lax.all_to_all(slots, "tm", 0, 0, tiled=True, axis_index_groups=groups).reshape(value.shape)


def shards(guess, forcing, coarse_gain, kernel_levels, kernel_code, settle_levels, settle_class):
    intervals = lax.axis_size("tm")
    rows = guess.reshape(SLICES, C, PLANES, ROWS, 128).transpose(1, 2, 3, 0, 4).reshape(C * OWN * SLICES, 128)
    slab = arr(C, OWN, 128)
    wide, four, three = (arr(C * n, 128) for n in (HALO + THREE, HALO, THREE))
    pieces, double = arr(GROUP * PIECE, 128), arr(GROUP * WIDE, 128)
    own, force, near, far = call(
        prep_kernel,
        [rows, forcing],
        [slab, slab, wide, wide],
        [pltpu.VMEM(rows.shape, F32), pltpu.VMEM(forcing.shape, F32), pltpu.SemaphoreType.DMA((2,))],
        [HBM] * 2,
        53.25,
    )
    near, far = exchange(near, far)
    small = (kernel_levels, kernel_code, settle_levels, settle_class)
    coefs = call(
        setup_kernel,
        list(small),
        [arr(C * C, 8, 128), arr(C, 8, 128), arr(3, 8, 128), arr(WIN // 8, 8, 128)],
        place=[SMEM] * len(small),
    )
    gain, spaced = call(gain_kernel, [coarse_gain], [pieces, arr(GROUP * SPACED, 128)])
    state, near, far, fwin = call(
        first_kernel,
        [own, force, far, near, *coefs],
        [slab, four, four, arr(C, WIN, 128)],
        WORK,
    )
    near, far = exchange(near, far)
    (element,) = call(second_kernel, [state, far, near, fwin, gain, *coefs], [double], WORK)
    spread = swap(element, 1, DOWN)
    sums, totals, tail = call(local_kernel, [spread, spaced], [pieces, pieces, arr(WIDE, 128)])
    totals = swap(totals, GROUP, MIDDLE)
    tail = lax.ppermute(tail, "tm", [(i, i + GROUP) for i in range(intervals - GROUP)])
    (back,) = call(prefix_kernel, [totals, tail, sums, spread, spaced], [double])
    back = swap(back, 1, DOWN)
    state, near, far = call(
        gather_kernel, [back, own], [slab, three, three]
    )
    near, far = exchange(near, far)
    updated, corr = call(
        last_kernel,
        [state, far, near, fwin, back, *coefs],
        [arr(C * OWN * SLICES, 128), arr(C * OWN, 128)],
        WORK,
    )
    updated = updated.reshape(C, PLANES, ROWS, SLICES, 128).transpose(3, 0, 1, 2, 4)
    return (
        updated.reshape(SLICES, C, PLANES, ROWS * 128),
        corr.reshape(1, C, PLANES, ROWS * 128),
    )


def solution(mesh):
    in_specs = (
        P("tm", None, "space", None),
        P(None, "space", None),
        P(None, "space", None),
        P(),
        P(),
        P(),
        P(),
    )
    out_specs = (P("tm", None, "space", None), P("tm", None, "space", None))
    return jax.shard_map(shards, mesh=mesh, in_specs=in_specs, out_specs=out_specs, check_vma=False)
```

```python
import functools

import jax
import jax.numpy as jnp
from jax import lax
from jax.experimental import pallas as pl
from jax.experimental.pallas import tpu as pltpu
from jax.sharding import PartitionSpec as P

F32 = jnp.float32
C = 12
NY = 16
NZ = 32
PLANES = 6
NX = 48
SLICES = 4
ROWS = 4
OWN = PLANES * ROWS
HALO = 4 * ROWS
THREE = 3 * ROWS
WIN = 64
BASE = 5 * ROWS
GROUP = 8
PIECE = C * OWN // GROUP
WIDE = 2 * PIECE
SPACED = 40
CHUNK = 12
VMEM = pl.BlockSpec(memory_space=pltpu.VMEM)
SMEM = pl.BlockSpec(memory_space=pltpu.SMEM)
HBM = pl.BlockSpec(memory_space=pl.ANY)


def arr(*shape):
    return jax.ShapeDtypeStruct(shape, F32)


def even_place():
    return lax.axis_index("space") % 2 == 0


def put_sends(first, last, near, far):
    even = even_place()

    @pl.when(even)
    def _():
        last(near)
        first(far)

    @pl.when(jnp.logical_not(even))
    def _():
        first(near)
        last(far)


def put_halo(buf, near, far, count, start):
    even = even_place()

    def put(src, row):
        for c in range(C):
            buf[c, row : row + count, :] = src[start + c * count : start + (c + 1) * count, :]

    @pl.when(even)
    def _():
        put(far, BASE - count)
        put(near, BASE + OWN)

    @pl.when(jnp.logical_not(even))
    def _():
        put(near, BASE - count)
        put(far, BASE + OWN)


def pack(src, row, count, start):
    def into(dst):
        for c in range(C):
            dst[start + c * count : start + (c + 1) * count, :] = src[c, row : row + count, :]

    return into


def take_guess(raw, own):
    for c in range(C):
        own[c] = raw[pl.ds(c * OWN * SLICES, OWN, stride=SLICES), :]


def to_rows(raw, rows, scale):
    for c in range(C):
        for r in range(ROWS):
            value = raw[c, :, 128 * r : 128 * r + 128]
            rows[pl.ds(c * OWN + r, PLANES, stride=ROWS), :] = value if scale is None else value * scale


def prep_kernel(guess, forcing, own, force, near, far, raw, fraw, frows, sems):
    one = pltpu.make_async_copy(forcing, fraw, sems.at[0])
    two = pltpu.make_async_copy(guess, raw, sems.at[1])
    one.start()
    two.start()
    one.wait()
    to_rows(fraw, frows, 0.1)
    for c in range(C):
        force[c] = frows[c * OWN : (c + 1) * OWN, :]
    two.wait()
    take_guess(raw, own)

    def first(dst):
        pack(own, 0, HALO, 0)(dst)
        pack(force, 0, THREE, C * HALO)(dst)

    def last(dst):
        pack(own, OWN - HALO, HALO, 0)(dst)
        pack(force, OWN - THREE, THREE, C * HALO)(dst)

    put_sends(first, last, near, far)


def gain_kernel(raw, rows, spaced, wide):
    to_rows(raw, wide, None)
    rows[...] = wide[: C * OWN, :]
    for p in range(GROUP):
        spaced[p * SPACED : p * SPACED + PIECE, :] = rows[p * PIECE : (p + 1) * PIECE, :]


def setup_kernel(lv, cd, st, kl, kv, wup, wfix, mask):
    lane = lax.broadcasted_iota(jnp.int32, (8, 128), 1)
    row = lax.broadcasted_iota(jnp.int32, (8, 128), 0)
    z = lane % NZ
    edge_row = row % ROWS
    for j in range(C):
        col = [lv[cd[i, j]] for i in range(C)]
        total = functools.reduce(lambda x, y: x + y, col)
        speed = st[kl[j]]
        for i in range(C):
            v = (col[i] - total) + (1.0 - 0.48) - speed if i == j else col[i]
            kv[i * C + j] = jnp.full((8, 128), v, F32)
        wup[j] = jnp.where(z < NZ - 1, 0.08 + speed, 0.0)
    wfix[0] = jnp.where(z > 0, F32(0.08), F32(0.0))
    wfix[1] = jnp.where(jnp.logical_and(lane >= 96, edge_row == ROWS - 1), F32(0.0), F32(0.08))
    wfix[2] = jnp.where(jnp.logical_and(lane < 32, edge_row == 0), F32(0.0), F32(0.08))
    start = lax.axis_index("space") * PLANES - 5
    for t in range(WIN // 8):
        plane = start + 2 * t + row // ROWS
        inside = jnp.logical_and(plane >= 0, plane < NX)
        mask[t] = jnp.where(inside, F32(1.0), F32(0.0))


def clear_edges(buf):
    z = jnp.zeros((C, 8, 128), F32)
    buf[:, 0:8, :] = z
    buf[:, WIN - 8 : WIN, :] = z


def block_step(src, dst, fwin, t, kv, wup, wfix, mask):
    lane = lax.broadcasted_iota(jnp.int32, (8, 128), 1)
    row = lax.broadcasted_iota(jnp.int32, (8, 128), 0)
    low = row < ROWS
    right = lane >= 96
    left = lane < 32
    wdn, wah, wbe = wfix[0], wfix[1], wfix[2]

    def rows(k):
        return pl.ds((t + k) * 8, 8)

    acc = []
    for i in range(C):
        p = [src[i, rows(k), :] for k in (-1, 0, 1, 2)]
        q = [pltpu.roll(v, 4, 0) for v in p]
        pair = []
        for k in (0, 1):
            c = p[k + 1]
            xs = q[k + 1] + jnp.where(low, q[k], q[k + 2])
            up = pltpu.roll(c, 127, 1)
            dn = pltpu.roll(c, 1, 1)
            ra = pltpu.roll(c, 96, 1)
            rb = pltpu.roll(c, 32, 1)
            ah = jnp.where(right, pltpu.roll(ra, 7, 0), ra)
            be = jnp.where(left, pltpu.roll(rb, 1, 0), rb)
            new = fwin[i, rows(k), :] + 0.08 * xs
            new = new + wup[i] * up
            new = new + wdn * dn
            new = new + wah * ah
            new = new + wbe * be
            pair.append(new)
        acc.append(pair)
    for j in range(C):
        c = [src[j, rows(k), :] for k in (0, 1)]
        for i in range(C):
            w = kv[i * C + j]
            acc[i] = [acc[i][k] + w * c[k] for k in (0, 1)]
    for k in (0, 1):
        m = mask[t + k]
        for i in range(C):
            dst[i, rows(k), :] = acc[i][k] * m


def steps(bufs, fwin, plan, coefs):
    for s, (first, count) in enumerate(plan):
        src, dst = bufs[s % 2], bufs[(s + 1) % 2]
        for b in range(count):
            block_step(src, dst, fwin, first + 2 * b, *coefs)


FOUR = ((1, 3), (1, 3), (2, 2), (2, 2))


def chunks():
    for t in range(C * OWN // CHUNK):
        c, x = divmod(t * CHUNK, OWN)
        p, r = divmod(t * CHUNK, PIECE)
        yield c, x, p, r


def first_kernel(own, force, far, near, kv, wup, wfix, mask, state, send_near, send_far, fwin, a, b):
    clear_edges(a)
    clear_edges(b)
    clear_edges(fwin)
    a[:, BASE : BASE + OWN, :] = own[...]
    fwin[:, BASE : BASE + OWN, :] = force[...]
    put_halo(a, near, far, HALO, 0)
    put_halo(fwin, near, far, THREE, C * HALO)
    steps((a, b), fwin, FOUR, (kv, wup, wfix, mask))
    state[...] = a[:, BASE : BASE + OWN, :]
    put_sends(pack(state, 0, HALO, 0), pack(state, OWN - HALO, HALO, 0), send_near, send_far)


def second_kernel(state, far, near, fwin, gain, kv, wup, wfix, mask, out, a, b):
    clear_edges(a)
    clear_edges(b)
    a[:, BASE : BASE + OWN, :] = state[...]
    put_halo(a, near, far, HALO, 0)
    steps((a, b), fwin, FOUR, (kv, wup, wfix, mask))
    use = jnp.where(lax.axis_index("tm") > 0, F32(1.0), F32(0.0))
    for c, x, p, r in chunks():
        u = state[c, x : x + CHUNK, :]
        v = a[c, BASE + x : BASE + x + CHUNK, :]
        row = p * WIDE + r
        out[row : row + CHUNK, :] = v - use * (gain[c * OWN + x : c * OWN + x + CHUNK, :] * u)
        out[row + PIECE : row + PIECE + CHUNK, :] = u


def my_gain(gain):
    place = GROUP - 1 - lax.axis_index("tm") % GROUP
    return gain[pl.ds(pl.multiple_of(place * SPACED, 8), PIECE), :]


def slot(i, width=PIECE, half=0):
    start = (GROUP - 1 - i) * width + half * PIECE
    return slice(start, start + PIECE)


def local_kernel(pieces, gain, sums, total, tail):
    mine = my_gain(gain)
    running = pieces[slot(0, WIDE), :]
    sums[slot(0), :] = running
    for i in range(1, GROUP):
        running = mine * running + pieces[slot(i, WIDE), :]
        sums[slot(i), :] = running
        if i == GROUP - 2:
            tail[:PIECE, :] = running
    tail[PIECE:, :] = pieces[slot(GROUP - 1, WIDE, 1), :]
    for i in range(GROUP):
        total[slot(i), :] = running


def prefix_kernel(totals, tail, sums, pieces, gain, out):
    group = lax.axis_index("tm") // GROUP
    g1 = my_gain(gain)
    g2 = g1 * g1
    g4 = g2 * g2
    g8 = g4 * g4
    before = jnp.zeros((PIECE, 128), F32)
    ahead = before
    for g in range(GROUP - 1):
        take = g < group
        ahead = jnp.where(take, before, ahead)
        before = jnp.where(take, g8 * before + totals[slot(g), :], before)
    for i in range(GROUP):
        if i == 0:
            base = tail[PIECE:, :]
            value = tail[:PIECE, :] + (g4 * g2 * g1) * ahead
        else:
            base = pieces[slot(i - 1, WIDE, 1), :]
            if i == 1:
                value = jnp.where(group > 0, before, base)
            else:
                before = g1 * before
                value = sums[slot(i - 2), :] + before
        out[slot(i, WIDE), :] = value
        out[slot(i, WIDE, 1), :] = value - base


def gather_kernel(pieces, own, state, near, far):
    first = lax.axis_index("tm") == 0

    @pl.when(first)
    def _():
        state[...] = own[...]

    @pl.when(jnp.logical_not(first))
    def _():
        for c, x, p, r in chunks():
            state[c, x : x + CHUNK, :] = pieces[p * WIDE + r : p * WIDE + r + CHUNK, :]

    put_sends(pack(state, 0, THREE, 0), pack(state, OWN - THREE, THREE, 0), near, far)


def last_kernel(state, far, near, fwin, pieces, kv, wup, wfix, mask, out, corr, a, b):
    clear_edges(a)
    clear_edges(b)
    a[:, BASE : BASE + OWN, :] = state[...]
    put_halo(a, near, far, THREE, 0)

    def emit(buf, j):
        for c in range(C):
            out[pl.ds(c * OWN * SLICES + j, OWN, stride=SLICES), :] = buf[c, BASE : BASE + OWN, :]

    emit(a, 0)
    bufs = (a, b)
    for j, one in enumerate(((1, 3), (2, 2), (2, 2))):
        src, dst = bufs[j % 2], bufs[(j + 1) % 2]
        steps((src, dst), fwin, (one,), (kv, wup, wfix, mask))
        emit(dst, j + 1)
    late = lax.axis_index("tm") >= 1
    for c, x, p, r in chunks():
        row, start = c * OWN + x, p * WIDE + PIECE + r
        corr[row : row + CHUNK, :] = jnp.where(late, pieces[start : start + CHUNK, :], 0.0)


ROOMY = pltpu.VMEM((C * OWN + 16, 128), F32)
WORK = [pltpu.VMEM((C, WIN, 128), F32), pltpu.VMEM((C, WIN, 128), F32)]


def call(kernel, ins, outs, scratch=(), place=None, grant=32):
    return pl.pallas_call(
        kernel,
        out_shape=outs,
        in_specs=place or [VMEM] * len(ins),
        out_specs=[VMEM] * len(outs),
        scratch_shapes=list(scratch),
        compiler_params=pltpu.CompilerParams(vmem_limit_bytes=int(grant * 1024 * 1024)),
        name=kernel.__name__,
    )(*ins)


def exchange(near, far):
    places = lax.axis_size("space")
    inner = [(i, i ^ 1) for i in range(places)]
    outer = [(i, j) for i in range(places) for j in [i - 1 if i % 2 == 0 else i + 1] if 0 <= j < places]
    far = lax.ppermute(far, "space", outer)
    near = lax.ppermute(near, "space", inner)
    return near, far


def swap(value, stride):
    count = lax.axis_size("tm")
    firsts = [i for i in range(count) if (i // stride) % GROUP == 0]
    groups = [[i + stride * j for j in reversed(range(GROUP))] for i in firsts]
    slots = value.reshape(GROUP, -1)
    return lax.all_to_all(slots, "tm", 0, 0, tiled=True, axis_index_groups=groups).reshape(value.shape)


def shards(guess, forcing, coarse_gain, kernel_levels, kernel_code, settle_levels, settle_class):
    intervals = lax.axis_size("tm")
    rows = guess.reshape(SLICES, C, PLANES, ROWS, 128).transpose(1, 2, 3, 0, 4).reshape(C * OWN * SLICES, 128)
    slab = arr(C, OWN, 128)
    wide, four, three = (arr(C * n, 128) for n in (HALO + THREE, HALO, THREE))
    pieces, double = arr(GROUP * PIECE, 128), arr(GROUP * WIDE, 128)
    own, force, near, far = call(
        prep_kernel,
        [rows, forcing],
        [slab, slab, wide, wide],
        [pltpu.VMEM(rows.shape, F32), pltpu.VMEM(forcing.shape, F32), ROOMY, pltpu.SemaphoreType.DMA((2,))],
        [HBM] * 2,
        53.25,
    )
    near, far = exchange(near, far)
    small = (kernel_levels, kernel_code, settle_levels, settle_class)
    coefs = call(
        setup_kernel,
        list(small),
        [arr(C * C, 8, 128), arr(C, 8, 128), arr(3, 8, 128), arr(WIN // 8, 8, 128)],
        place=[SMEM] * len(small),
    )
    gain, spaced = call(gain_kernel, [coarse_gain], [pieces, arr(GROUP * SPACED, 128)], [ROOMY])
    state, near, far, fwin = call(
        first_kernel,
        [own, force, far, near, *coefs],
        [slab, four, four, arr(C, WIN, 128)],
        WORK,
    )
    near, far = exchange(near, far)
    (element,) = call(second_kernel, [state, far, near, fwin, gain, *coefs], [double], WORK)
    spread = swap(element, 1)
    sums, totals, tail = call(local_kernel, [spread, spaced], [pieces, pieces, arr(WIDE, 128)])
    totals = swap(totals, GROUP)
    tail = lax.ppermute(tail, "tm", [(i, i + GROUP) for i in range(intervals - GROUP)])
    (back,) = call(prefix_kernel, [totals, tail, sums, spread, spaced], [double])
    back = swap(back, 1)
    state, near, far = call(
        gather_kernel, [back, own], [slab, three, three]
    )
    near, far = exchange(near, far)
    updated, corr = call(
        last_kernel,
        [state, far, near, fwin, back, *coefs],
        [arr(C * OWN * SLICES, 128), arr(C * OWN, 128)],
        WORK,
    )
    updated = updated.reshape(C, PLANES, ROWS, SLICES, 128).transpose(3, 0, 1, 2, 4)
    return (
        updated.reshape(SLICES, C, PLANES, ROWS * 128),
        corr.reshape(1, C, PLANES, ROWS * 128),
    )


def solution(mesh):
    in_specs = (
        P("tm", None, "space", None),
        P(None, "space", None),
        P(None, "space", None),
        P(),
        P(),
        P(),
        P(),
    )
    out_specs = (P("tm", None, "space", None), P("tm", None, "space", None))
    return jax.shard_map(shards, mesh=mesh, in_specs=in_specs, out_specs=out_specs, check_vma=False)
```

```python
import functools

import jax
import jax.numpy as jnp
from jax import lax
from jax.experimental import pallas as pl
from jax.experimental.pallas import tpu as pltpu
from jax.sharding import PartitionSpec as P

F32 = jnp.float32
C = 12
NY = 16
NZ = 32
PLANES = 6
NX = 48
SLICES = 4
DIFFUSION = 0.08
ROWS = 4
OWN = PLANES * ROWS
HALO = 4 * ROWS
THREE = 3 * ROWS
WIN = 64
BASE = 5 * ROWS
GROUP = 8
PIECE = C * OWN // GROUP
WIDE = 2 * PIECE
SPACED = 40
CHUNK = 12
VMEM = pl.BlockSpec(memory_space=pltpu.VMEM)
SMEM = pl.BlockSpec(memory_space=pltpu.SMEM)
HBM = pl.BlockSpec(memory_space=pl.ANY)


def arr(*shape):
    return jax.ShapeDtypeStruct(shape, F32)


def even_place():
    return lax.axis_index("space") % 2 == 0


def put_sends(first, last, near, far):
    even = even_place()

    @pl.when(even)
    def _():
        last(near)
        first(far)

    @pl.when(jnp.logical_not(even))
    def _():
        first(near)
        last(far)


def put_halo(buf, near, far, count, start):
    even = even_place()

    def put(src, row):
        for c in range(C):
            buf[c, row : row + count, :] = src[start + c * count : start + (c + 1) * count, :]

    @pl.when(even)
    def _():
        put(far, BASE - count)
        put(near, BASE + OWN)

    @pl.when(jnp.logical_not(even))
    def _():
        put(near, BASE - count)
        put(far, BASE + OWN)


def pack(src, row, count, start):
    def into(dst):
        for c in range(C):
            dst[start + c * count : start + (c + 1) * count, :] = src[c, row : row + count, :]

    return into


def take_guess(raw, own, classes):
    for c in classes:
        own[c] = raw[pl.ds(c * OWN * SLICES, OWN, stride=SLICES), :]


def to_rows(raw, rows, scale):
    for c in range(C):
        for r in range(ROWS):
            value = raw[c, :, 128 * r : 128 * r + 128]
            rows[pl.ds(c * OWN + r, PLANES, stride=ROWS), :] = value if scale is None else value * scale


def prep_kernel(guess, forcing, own, force, near, far, raw, fraw, frows, sems):
    size = C * OWN * SLICES // 2
    halves = [pl.ds(n * size, size) for n in (0, 1)]
    one = pltpu.make_async_copy(forcing, fraw, sems.at[0])
    parts = [pltpu.make_async_copy(guess.at[h], raw.at[h], sems.at[n + 1]) for n, h in enumerate(halves)]
    one.start()
    for part in parts:
        part.start()
    one.wait()
    to_rows(fraw, frows, 0.1 / DIFFUSION)
    for c in range(C):
        force[c] = frows[c * OWN : (c + 1) * OWN, :]
    for n, part in enumerate(parts):
        part.wait()
        take_guess(raw, own, range(n * C // 2, (n + 1) * C // 2))

    def first(dst):
        pack(own, 0, HALO, 0)(dst)
        pack(force, 0, THREE, C * HALO)(dst)

    def last(dst):
        pack(own, OWN - HALO, HALO, 0)(dst)
        pack(force, OWN - THREE, THREE, C * HALO)(dst)

    put_sends(first, last, near, far)


def gain_kernel(raw, rows, spaced, wide):
    to_rows(raw, wide, None)
    rows[...] = wide[: C * OWN, :]
    for p in range(GROUP):
        spaced[p * SPACED : p * SPACED + PIECE, :] = rows[p * PIECE : (p + 1) * PIECE, :]


def setup_kernel(lv, cd, st, kl, kv, wup, wfix, mask):
    lane = lax.broadcasted_iota(jnp.int32, (8, 128), 1)
    row = lax.broadcasted_iota(jnp.int32, (8, 128), 0)
    z = lane % NZ
    edge_row = row % ROWS
    for j in range(C):
        col = [lv[cd[i, j]] for i in range(C)]
        total = functools.reduce(lambda x, y: x + y, col)
        speed = st[kl[j]]
        for i in range(C):
            v = (col[i] - total) + (1.0 - 6.0 * DIFFUSION) - speed if i == j else col[i]
            kv[i * C + j] = jnp.full((8, 128), v * (1.0 / DIFFUSION), F32)
        wup[j] = jnp.where(z < NZ - 1, 1.0 + speed * (1.0 / DIFFUSION), 0.0)
    wfix[0] = jnp.where(z > 0, F32(1.0), F32(0.0))
    wfix[1] = jnp.where(jnp.logical_and(lane >= 96, edge_row == ROWS - 1), F32(0.0), F32(1.0))
    wfix[2] = jnp.where(jnp.logical_and(lane < 32, edge_row == 0), F32(0.0), F32(1.0))
    start = lax.axis_index("space") * PLANES - 5
    for t in range(WIN // 8):
        plane = start + 2 * t + row // ROWS
        inside = jnp.logical_and(plane >= 0, plane < NX)
        mask[t] = jnp.where(inside, F32(DIFFUSION), F32(0.0))


def clear_edges(buf):
    z = jnp.zeros((C, 8, 128), F32)
    buf[:, 0:8, :] = z
    buf[:, WIN - 8 : WIN, :] = z


def block_step(src, dst, fwin, t, classes, kv, wup, wfix, mask):
    lane = lax.broadcasted_iota(jnp.int32, (8, 128), 1)
    row = lax.broadcasted_iota(jnp.int32, (8, 128), 0)
    low = row < ROWS
    right = lane >= 96
    left = lane < 32
    wdn, wah, wbe = wfix[0], wfix[1], wfix[2]

    def rows(k):
        return pl.ds((t + k) * 8, 8)

    acc = {}
    for i in classes:
        p = [src[i, rows(k), :] for k in (-1, 0, 1, 2)]
        q = [pltpu.roll(v, 4, 0) for v in p]
        pair = []
        for k in (0, 1):
            c = p[k + 1]
            xs = q[k + 1] + jnp.where(low, q[k], q[k + 2])
            up = pltpu.roll(c, 127, 1)
            dn = pltpu.roll(c, 1, 1)
            ra = pltpu.roll(c, 96, 1)
            rb = pltpu.roll(c, 32, 1)
            ah = jnp.where(right, pltpu.roll(ra, 7, 0), ra)
            be = jnp.where(left, pltpu.roll(rb, 1, 0), rb)
            new = fwin[i, rows(k), :] + xs
            new = new + wup[i] * up
            new = new + wdn * dn
            new = new + wah * ah
            new = new + wbe * be
            pair.append(new)
        acc[i] = pair
    for j in range(C):
        c = [src[j, rows(k), :] for k in (0, 1)]
        for i in classes:
            w = kv[i * C + j]
            acc[i] = [acc[i][k] + w * c[k] for k in (0, 1)]
    for k in (0, 1):
        m = mask[t + k]
        for i in classes:
            dst[i, rows(k), :] = acc[i][k] * m


def steps(bufs, fwin, plan, coefs, classes=range(C)):
    for s, (first, count) in enumerate(plan):
        src, dst = bufs[s % 2], bufs[(s + 1) % 2]
        for b in range(count):
            block_step(src, dst, fwin, first + 2 * b, classes, *coefs)


FOUR = ((1, 3), (1, 3), (2, 2), (2, 2))


def chunks():
    for t in range(C * OWN // CHUNK):
        c, x = divmod(t * CHUNK, OWN)
        p, r = divmod(t * CHUNK, PIECE)
        yield c, x, p, r


def first_kernel(own, force, far, near, kv, wup, wfix, mask, state, send_near, send_far, fwin, a, b):
    clear_edges(a)
    clear_edges(b)
    clear_edges(fwin)
    a[:, BASE : BASE + OWN, :] = own[...]
    fwin[:, BASE : BASE + OWN, :] = force[...]
    put_halo(a, near, far, HALO, 0)
    put_halo(fwin, near, far, THREE, C * HALO)
    steps((a, b), fwin, FOUR, (kv, wup, wfix, mask))
    state[...] = a[:, BASE : BASE + OWN, :]
    put_sends(pack(state, 0, HALO, 0), pack(state, OWN - HALO, HALO, 0), send_near, send_far)


def second_kernel(state, far, near, fwin, gain, kv, wup, wfix, mask, out, a, b):
    clear_edges(a)
    clear_edges(b)
    a[:, BASE : BASE + OWN, :] = state[...]
    put_halo(a, near, far, HALO, 0)
    steps((a, b), fwin, FOUR, (kv, wup, wfix, mask))
    use = jnp.where(lax.axis_index("tm") > 0, F32(1.0), F32(0.0))
    for c, x, p, r in chunks():
        u = state[c, x : x + CHUNK, :]
        v = a[c, BASE + x : BASE + x + CHUNK, :]
        row = p * WIDE + r
        out[row : row + CHUNK, :] = v - use * (gain[c * OWN + x : c * OWN + x + CHUNK, :] * u)
        out[row + PIECE : row + PIECE + CHUNK, :] = u


def my_gain(gain):
    place = GROUP - 1 - lax.axis_index("tm") % GROUP
    return gain[pl.ds(pl.multiple_of(place * SPACED, 8), PIECE), :]


def slot(i, width=PIECE, half=0):
    start = (GROUP - 1 - i) * width + half * PIECE
    return slice(start, start + PIECE)


def local_kernel(pieces, gain, sums, total, tail):
    mine = my_gain(gain)
    running = pieces[slot(0, WIDE), :]
    sums[slot(0), :] = running
    for i in range(1, GROUP):
        running = mine * running + pieces[slot(i, WIDE), :]
        sums[slot(i), :] = running
        if i == GROUP - 2:
            tail[:PIECE, :] = running
    tail[PIECE:, :] = pieces[slot(GROUP - 1, WIDE, 1), :]
    for i in range(GROUP):
        total[slot(i), :] = running


def prefix_kernel(totals, tail, sums, pieces, gain, out):
    group = lax.axis_index("tm") // GROUP
    g1 = my_gain(gain)
    g2 = g1 * g1
    g4 = g2 * g2
    g8 = g4 * g4
    before = jnp.zeros((PIECE, 128), F32)
    ahead = before
    for g in range(GROUP - 1):
        take = g < group
        ahead = jnp.where(take, before, ahead)
        before = jnp.where(take, g8 * before + totals[slot(g), :], before)
    for i in range(GROUP):
        if i == 0:
            base = tail[PIECE:, :]
            value = tail[:PIECE, :] + (g4 * g2 * g1) * ahead
        else:
            base = pieces[slot(i - 1, WIDE, 1), :]
            if i == 1:
                value = jnp.where(group > 0, before, base)
            else:
                before = g1 * before
                value = sums[slot(i - 2), :] + before
        out[slot(i, WIDE), :] = value
        out[slot(i, WIDE, 1), :] = value - base


def gather_kernel(pieces, own, state, near, far):
    first = lax.axis_index("tm") == 0

    @pl.when(first)
    def _():
        state[...] = own[...]

    @pl.when(jnp.logical_not(first))
    def _():
        for c, x, p, r in chunks():
            state[c, x : x + CHUNK, :] = pieces[p * WIDE + r : p * WIDE + r + CHUNK, :]

    put_sends(pack(state, 0, THREE, 0), pack(state, OWN - THREE, THREE, 0), near, far)


def last_kernel(state, far, near, fwin, pieces, kv, wup, wfix, mask, out, corr, a, b, held, fixed, sems):
    late = lax.axis_index("tm") >= 1
    for c, x, p, r in chunks():
        row, start = c * OWN + x, p * WIDE + PIECE + r
        fixed[row : row + CHUNK, :] = jnp.where(late, pieces[start : start + CHUNK, :], 0.0)
    copies = [pltpu.make_async_copy(fixed, corr, sems.at[0])]
    copies[0].start()
    clear_edges(a)
    clear_edges(b)
    a[:, BASE : BASE + OWN, :] = state[...]
    put_halo(a, near, far, THREE, 0)
    coefs = (kv, wup, wfix, mask)

    def emit(buf, j, classes=range(C)):
        for c in classes:
            held[pl.ds(c * OWN * SLICES + j, OWN, stride=SLICES), :] = buf[c, BASE : BASE + OWN, :]

    emit(a, 0)
    steps((a, b), fwin, ((1, 3),), coefs)
    emit(b, 1)
    steps((b, a), fwin, ((2, 2),), coefs)
    emit(a, 2)
    for n in (0, 1):
        classes = range(n * C // 2, (n + 1) * C // 2)
        steps((a, b), fwin, ((2, 2),), coefs, classes)
        emit(b, 3, classes)
        size = C * OWN * SLICES // 2
        half = pl.ds(n * size, size)
        copies.append(pltpu.make_async_copy(held.at[half], out.at[half], sems.at[n + 1]))
        copies[-1].start()
    for one in copies:
        one.wait()


ROOMY = pltpu.VMEM((C * OWN + 16, 128), F32)
WORK = [pltpu.VMEM((C, WIN, 128), F32), pltpu.VMEM((C, WIN, 128), F32)]


def call(kernel, ins, outs, scratch=(), place=None, grant=32, results=VMEM):
    return pl.pallas_call(
        kernel,
        out_shape=outs,
        in_specs=place or [VMEM] * len(ins),
        out_specs=[results] * len(outs),
        scratch_shapes=list(scratch),
        compiler_params=pltpu.CompilerParams(vmem_limit_bytes=int(grant * 1024 * 1024)),
        name=kernel.__name__,
    )(*ins)


def exchange(near, far):
    places = lax.axis_size("space")
    inner = [(i, i ^ 1) for i in range(places)]
    outer = [(i, j) for i in range(places) for j in [i - 1 if i % 2 == 0 else i + 1] if 0 <= j < places]
    far = lax.ppermute(far, "space", outer)
    near = lax.ppermute(near, "space", inner)
    return near, far


def swap(value, stride):
    count = lax.axis_size("tm")
    firsts = [i for i in range(count) if (i // stride) % GROUP == 0]
    groups = [[i + stride * j for j in reversed(range(GROUP))] for i in firsts]
    slots = value.reshape(GROUP, -1)
    return lax.all_to_all(slots, "tm", 0, 0, tiled=True, axis_index_groups=groups).reshape(value.shape)


def shards(guess, forcing, coarse_gain, kernel_levels, kernel_code, settle_levels, settle_class):
    intervals = lax.axis_size("tm")
    rows = guess.reshape(SLICES, C, PLANES, ROWS, 128).transpose(1, 2, 3, 0, 4).reshape(C * OWN * SLICES, 128)
    slab = arr(C, OWN, 128)
    wide, four, three = (arr(C * n, 128) for n in (HALO + THREE, HALO, THREE))
    pieces, double = arr(GROUP * PIECE, 128), arr(GROUP * WIDE, 128)
    own, force, near, far = call(
        prep_kernel,
        [rows, forcing],
        [slab, slab, wide, wide],
        [pltpu.VMEM(rows.shape, F32), pltpu.VMEM(forcing.shape, F32), ROOMY, pltpu.SemaphoreType.DMA((3,))],
        [HBM] * 2,
        53.25,
    )
    near, far = exchange(near, far)
    small = (kernel_levels, kernel_code, settle_levels, settle_class)
    coefs = call(
        setup_kernel,
        list(small),
        [arr(C * C, 8, 128), arr(C, 8, 128), arr(3, 8, 128), arr(WIN // 8, 8, 128)],
        place=[SMEM] * len(small),
    )
    gain, spaced = call(gain_kernel, [coarse_gain], [pieces, arr(GROUP * SPACED, 128)], [ROOMY])
    state, near, far, fwin = call(
        first_kernel,
        [own, force, far, near, *coefs],
        [slab, four, four, arr(C, WIN, 128)],
        WORK,
    )
    near, far = exchange(near, far)
    (element,) = call(second_kernel, [state, far, near, fwin, gain, *coefs], [double], WORK)
    spread = swap(element, 1)
    sums, totals, tail = call(local_kernel, [spread, spaced], [pieces, pieces, arr(WIDE, 128)])
    totals = swap(totals, GROUP)
    tail = lax.ppermute(tail, "tm", [(i, i + GROUP) for i in range(intervals - GROUP)])
    (back,) = call(prefix_kernel, [totals, tail, sums, spread, spaced], [double])
    back = swap(back, 1)
    state, near, far = call(
        gather_kernel, [back, own], [slab, three, three]
    )
    near, far = exchange(near, far)
    sizes = (C * OWN * SLICES, 128), (C * OWN, 128)
    updated, corr = call(
        last_kernel,
        [state, far, near, fwin, back, *coefs],
        [arr(*size) for size in sizes],
        WORK + [pltpu.VMEM(size, F32) for size in sizes] + [pltpu.SemaphoreType.DMA((3,))],
        results=HBM,
    )
    updated = updated.reshape(C, PLANES, ROWS, SLICES, 128).transpose(3, 0, 1, 2, 4)
    return (
        updated.reshape(SLICES, C, PLANES, ROWS * 128),
        corr.reshape(1, C, PLANES, ROWS * 128),
    )


def solution(mesh):
    in_specs = (
        P("tm", None, "space", None),
        P(None, "space", None),
        P(None, "space", None),
        P(),
        P(),
        P(),
        P(),
    )
    out_specs = (P("tm", None, "space", None), P("tm", None, "space", None))
    return jax.shard_map(shards, mesh=mesh, in_specs=in_specs, out_specs=out_specs, check_vma=False)
```

```python
import functools

import jax
import jax.numpy as jnp
from jax import lax
from jax.experimental import pallas as pl
from jax.experimental.pallas import tpu as pltpu
from jax.sharding import PartitionSpec as P

F32 = jnp.float32
C = 12
NY = 16
NZ = 32
PLANES = 6
NX = 48
SLICES = 4
ROWS = 4
OWN = PLANES * ROWS
HALO = 4 * ROWS
THREE = 3 * ROWS
WIN = 64
BASE = 5 * ROWS
GROUP = 8
DOWN = (7, 3, 4, 0, 5, 1, 6, 2)
PIECE = C * OWN // GROUP
WIDE = 2 * PIECE
SPACED = 40
CHUNK = 12
VMEM = pl.BlockSpec(memory_space=pltpu.VMEM)
SMEM = pl.BlockSpec(memory_space=pltpu.SMEM)
HBM = pl.BlockSpec(memory_space=pl.ANY)


def arr(*shape):
    return jax.ShapeDtypeStruct(shape, F32)


def even_place():
    return lax.axis_index("space") % 2 == 0


def put_sends(first, last, near, far):
    even = even_place()

    @pl.when(even)
    def _():
        last(near)
        first(far)

    @pl.when(jnp.logical_not(even))
    def _():
        first(near)
        last(far)


def put_halo(buf, near, far, count, start):
    even = even_place()

    def put(src, row):
        for c in range(C):
            buf[c, row : row + count, :] = src[start + c * count : start + (c + 1) * count, :]

    @pl.when(even)
    def _():
        put(far, BASE - count)
        put(near, BASE + OWN)

    @pl.when(jnp.logical_not(even))
    def _():
        put(near, BASE - count)
        put(far, BASE + OWN)


def pack(src, row, count, start):
    def into(dst):
        for c in range(C):
            dst[start + c * count : start + (c + 1) * count, :] = src[c, row : row + count, :]

    return into


def take_guess(raw, own):
    for c in range(C):
        own[c] = raw[pl.ds(c * OWN * SLICES, OWN, stride=SLICES), :]


def to_rows(raw, rows, scale):
    for c in range(C):
        for r in range(ROWS):
            value = raw[c, :, 128 * r : 128 * r + 128]
            rows[pl.ds(c * OWN + r, PLANES, stride=ROWS), :] = value if scale is None else value * scale


def prep_kernel(guess, forcing, own, force, near, far, raw, fraw, frows, sems):
    one = pltpu.make_async_copy(forcing, fraw, sems.at[0])
    two = pltpu.make_async_copy(guess, raw, sems.at[1])
    one.start()
    two.start()
    one.wait()
    to_rows(fraw, frows, 0.1)
    for c in range(C):
        force[c] = frows[c * OWN : (c + 1) * OWN, :]
    two.wait()
    take_guess(raw, own)

    def first(dst):
        pack(own, 0, HALO, 0)(dst)
        pack(force, 0, THREE, C * HALO)(dst)

    def last(dst):
        pack(own, OWN - HALO, HALO, 0)(dst)
        pack(force, OWN - THREE, THREE, C * HALO)(dst)

    put_sends(first, last, near, far)


def gain_kernel(raw, rows, spaced, wide):
    to_rows(raw, wide, None)
    rows[...] = wide[: C * OWN, :]
    for p in range(GROUP):
        spaced[p * SPACED : p * SPACED + PIECE, :] = rows[p * PIECE : (p + 1) * PIECE, :]


def setup_kernel(lv, cd, st, kl, kv, wup, wfix, mask):
    lane = lax.broadcasted_iota(jnp.int32, (8, 128), 1)
    row = lax.broadcasted_iota(jnp.int32, (8, 128), 0)
    z = lane % NZ
    edge_row = row % ROWS
    for j in range(C):
        col = [lv[cd[i, j]] for i in range(C)]
        total = functools.reduce(lambda x, y: x + y, col)
        speed = st[kl[j]]
        for i in range(C):
            v = (col[i] - total) + (1.0 - 0.48) - speed if i == j else col[i]
            kv[i * C + j] = jnp.full((8, 128), v, F32)
        wup[j] = jnp.where(z < NZ - 1, 0.08 + speed, 0.0)
    wfix[0] = jnp.where(z > 0, F32(0.08), F32(0.0))
    wfix[1] = jnp.where(jnp.logical_and(lane >= 96, edge_row == ROWS - 1), F32(0.0), F32(0.08))
    wfix[2] = jnp.where(jnp.logical_and(lane < 32, edge_row == 0), F32(0.0), F32(0.08))
    start = lax.axis_index("space") * PLANES - 5
    for t in range(WIN // 8):
        plane = start + 2 * t + row // ROWS
        inside = jnp.logical_and(plane >= 0, plane < NX)
        mask[t] = jnp.where(inside, F32(1.0), F32(0.0))


def clear_edges(buf):
    z = jnp.zeros((C, 8, 128), F32)
    buf[:, 0:8, :] = z
    buf[:, WIN - 8 : WIN, :] = z


def block_step(src, dst, fwin, t, kv, wup, wfix, mask):
    lane = lax.broadcasted_iota(jnp.int32, (8, 128), 1)
    row = lax.broadcasted_iota(jnp.int32, (8, 128), 0)
    low = row < ROWS
    right = lane >= 96
    left = lane < 32
    wdn, wah, wbe = wfix[0], wfix[1], wfix[2]

    def rows(k):
        return pl.ds((t + k) * 8, 8)

    acc = []
    for i in range(C):
        p = [src[i, rows(k), :] for k in (-1, 0, 1, 2)]
        q = [pltpu.roll(v, 4, 0) for v in p]
        pair = []
        for k in (0, 1):
            c = p[k + 1]
            xs = q[k + 1] + jnp.where(low, q[k], q[k + 2])
            up = pltpu.roll(c, 127, 1)
            dn = pltpu.roll(c, 1, 1)
            ra = pltpu.roll(c, 96, 1)
            rb = pltpu.roll(c, 32, 1)
            ah = jnp.where(right, pltpu.roll(ra, 7, 0), ra)
            be = jnp.where(left, pltpu.roll(rb, 1, 0), rb)
            new = fwin[i, rows(k), :] + 0.08 * xs
            new = new + wup[i] * up
            new = new + wdn * dn
            new = new + wah * ah
            new = new + wbe * be
            pair.append(new)
        acc.append(pair)
    for j in range(C):
        c = [src[j, rows(k), :] for k in (0, 1)]
        for i in range(C):
            w = kv[i * C + j]
            acc[i] = [acc[i][k] + w * c[k] for k in (0, 1)]
    for k in (0, 1):
        m = mask[t + k]
        for i in range(C):
            dst[i, rows(k), :] = acc[i][k] * m


def steps(bufs, fwin, plan, coefs):
    for s, (first, count) in enumerate(plan):
        src, dst = bufs[s % 2], bufs[(s + 1) % 2]
        for b in range(count):
            block_step(src, dst, fwin, first + 2 * b, *coefs)


FOUR = ((1, 3), (1, 3), (2, 2), (2, 2))


def chunks():
    for t in range(C * OWN // CHUNK):
        c, x = divmod(t * CHUNK, OWN)
        p, r = divmod(t * CHUNK, PIECE)
        yield c, x, p, r


def first_kernel(own, force, far, near, kv, wup, wfix, mask, state, send_near, send_far, fwin, a, b):
    clear_edges(a)
    clear_edges(b)
    clear_edges(fwin)
    a[:, BASE : BASE + OWN, :] = own[...]
    fwin[:, BASE : BASE + OWN, :] = force[...]
    put_halo(a, near, far, HALO, 0)
    put_halo(fwin, near, far, THREE, C * HALO)
    steps((a, b), fwin, FOUR, (kv, wup, wfix, mask))
    state[...] = a[:, BASE : BASE + OWN, :]
    put_sends(pack(state, 0, HALO, 0), pack(state, OWN - HALO, HALO, 0), send_near, send_far)


def second_kernel(state, far, near, fwin, gain, kv, wup, wfix, mask, out, a, b):
    clear_edges(a)
    clear_edges(b)
    a[:, BASE : BASE + OWN, :] = state[...]
    put_halo(a, near, far, HALO, 0)
    steps((a, b), fwin, FOUR, (kv, wup, wfix, mask))
    use = jnp.where(lax.axis_index("tm") > 0, F32(1.0), F32(0.0))
    for c, x, p, r in chunks():
        u = state[c, x : x + CHUNK, :]
        v = a[c, BASE + x : BASE + x + CHUNK, :]
        row = p * WIDE + r
        out[row : row + CHUNK, :] = v - use * (gain[c * OWN + x : c * OWN + x + CHUNK, :] * u)
        out[row + PIECE : row + PIECE + CHUNK, :] = u


def my_gain(gain):
    member = lax.axis_index("tm") % GROUP
    place = sum(jnp.where(member == i, at, 0) for at, i in enumerate(DOWN))
    return gain[pl.ds(pl.multiple_of(place * SPACED, 8), PIECE), :]


def slot(i, width=PIECE, half=0):
    start = DOWN.index(i) * width + half * PIECE
    return slice(start, start + PIECE)


def local_kernel(pieces, gain, sums, total, tail):
    mine = my_gain(gain)
    running = pieces[slot(0, WIDE), :]
    sums[slot(0), :] = running
    for i in range(1, GROUP):
        running = mine * running + pieces[slot(i, WIDE), :]
        sums[slot(i), :] = running
        if i == GROUP - 2:
            tail[:PIECE, :] = running
    tail[PIECE:, :] = pieces[slot(GROUP - 1, WIDE, 1), :]
    for i in range(GROUP):
        total[i * PIECE : (i + 1) * PIECE, :] = running


def prefix_kernel(totals, tail, sums, pieces, gain, out):
    group = lax.axis_index("tm") // GROUP
    g1 = my_gain(gain)
    g2 = g1 * g1
    g4 = g2 * g2
    g8 = g4 * g4
    before = jnp.zeros((PIECE, 128), F32)
    ahead = before
    for g in range(GROUP - 1):
        take = g < group
        ahead = jnp.where(take, before, ahead)
        before = jnp.where(take, g8 * before + totals[(GROUP - 1 - g) * PIECE : (GROUP - g) * PIECE, :], before)
    for i in range(GROUP):
        if i == 0:
            base = tail[PIECE:, :]
            value = tail[:PIECE, :] + (g4 * g2 * g1) * ahead
        else:
            base = pieces[slot(i - 1, WIDE, 1), :]
            if i == 1:
                value = jnp.where(group > 0, before, base)
            else:
                before = g1 * before
                value = sums[slot(i - 2), :] + before
        out[slot(i, WIDE), :] = value
        out[slot(i, WIDE, 1), :] = value - base


def gather_kernel(pieces, own, state, near, far):
    first = lax.axis_index("tm") == 0

    @pl.when(first)
    def _():
        state[...] = own[...]

    @pl.when(jnp.logical_not(first))
    def _():
        for c, x, p, r in chunks():
            state[c, x : x + CHUNK, :] = pieces[p * WIDE + r : p * WIDE + r + CHUNK, :]

    put_sends(pack(state, 0, THREE, 0), pack(state, OWN - THREE, THREE, 0), near, far)


def last_kernel(state, far, near, fwin, pieces, kv, wup, wfix, mask, out, corr, a, b):
    clear_edges(a)
    clear_edges(b)
    a[:, BASE : BASE + OWN, :] = state[...]
    put_halo(a, near, far, THREE, 0)

    def emit(buf, j):
        for c in range(C):
            out[pl.ds(c * OWN * SLICES + j, OWN, stride=SLICES), :] = buf[c, BASE : BASE + OWN, :]

    emit(a, 0)
    bufs = (a, b)
    for j, one in enumerate(((1, 3), (2, 2), (2, 2))):
        src, dst = bufs[j % 2], bufs[(j + 1) % 2]
        steps((src, dst), fwin, (one,), (kv, wup, wfix, mask))
        emit(dst, j + 1)
    late = lax.axis_index("tm") >= 1
    for c, x, p, r in chunks():
        row, start = c * OWN + x, p * WIDE + PIECE + r
        corr[row : row + CHUNK, :] = jnp.where(late, pieces[start : start + CHUNK, :], 0.0)


ROOMY = pltpu.VMEM((C * OWN + 16, 128), F32)
WORK = [pltpu.VMEM((C, WIN, 128), F32), pltpu.VMEM((C, WIN, 128), F32)]


def call(kernel, ins, outs, scratch=(), place=None, grant=32):
    return pl.pallas_call(
        kernel,
        out_shape=outs,
        in_specs=place or [VMEM] * len(ins),
        out_specs=[VMEM] * len(outs),
        scratch_shapes=list(scratch),
        compiler_params=pltpu.CompilerParams(vmem_limit_bytes=int(grant * 1024 * 1024)),
        name=kernel.__name__,
    )(*ins)


def exchange(near, far):
    places = lax.axis_size("space")
    inner = [(i, i ^ 1) for i in range(places)]
    outer = [(i, j) for i in range(places) for j in [i - 1 if i % 2 == 0 else i + 1] if 0 <= j < places]
    far = lax.ppermute(far, "space", outer)
    near = lax.ppermute(near, "space", inner)
    return near, far


def swap(value, stride):
    count = lax.axis_size("tm")
    firsts = [i for i in range(count) if (i // stride) % GROUP == 0]
    groups = [[i + stride * j for j in (DOWN if stride == 1 else reversed(range(GROUP)))] for i in firsts]
    slots = value.reshape(GROUP, -1)
    return lax.all_to_all(slots, "tm", 0, 0, tiled=True, axis_index_groups=groups).reshape(value.shape)


def shards(guess, forcing, coarse_gain, kernel_levels, kernel_code, settle_levels, settle_class):
    intervals = lax.axis_size("tm")
    rows = guess.reshape(SLICES, C, PLANES, ROWS, 128).transpose(1, 2, 3, 0, 4).reshape(C * OWN * SLICES, 128)
    slab = arr(C, OWN, 128)
    wide, four, three = (arr(C * n, 128) for n in (HALO + THREE, HALO, THREE))
    pieces, double = arr(GROUP * PIECE, 128), arr(GROUP * WIDE, 128)
    own, force, near, far = call(
        prep_kernel,
        [rows, forcing],
        [slab, slab, wide, wide],
        [pltpu.VMEM(rows.shape, F32), pltpu.VMEM(forcing.shape, F32), ROOMY, pltpu.SemaphoreType.DMA((2,))],
        [HBM] * 2,
        53.25,
    )
    near, far = exchange(near, far)
    small = (kernel_levels, kernel_code, settle_levels, settle_class)
    coefs = call(
        setup_kernel,
        list(small),
        [arr(C * C, 8, 128), arr(C, 8, 128), arr(3, 8, 128), arr(WIN // 8, 8, 128)],
        place=[SMEM] * len(small),
    )
    gain, spaced = call(gain_kernel, [coarse_gain], [pieces, arr(GROUP * SPACED, 128)], [ROOMY])
    state, near, far, fwin = call(
        first_kernel,
        [own, force, far, near, *coefs],
        [slab, four, four, arr(C, WIN, 128)],
        WORK,
    )
    near, far = exchange(near, far)
    (element,) = call(second_kernel, [state, far, near, fwin, gain, *coefs], [double], WORK)
    spread = swap(element, 1)
    sums, totals, tail = call(local_kernel, [spread, spaced], [pieces, pieces, arr(WIDE, 128)])
    totals = swap(totals, GROUP)
    tail = lax.ppermute(tail, "tm", [(i, i + GROUP) for i in range(intervals - GROUP)])
    (back,) = call(prefix_kernel, [totals, tail, sums, spread, spaced], [double])
    back = swap(back, 1)
    state, near, far = call(
        gather_kernel, [back, own], [slab, three, three]
    )
    near, far = exchange(near, far)
    updated, corr = call(
        last_kernel,
        [state, far, near, fwin, back, *coefs],
        [arr(C * OWN * SLICES, 128), arr(C * OWN, 128)],
        WORK,
    )
    updated = updated.reshape(C, PLANES, ROWS, SLICES, 128).transpose(3, 0, 1, 2, 4)
    return (
        updated.reshape(SLICES, C, PLANES, ROWS * 128),
        corr.reshape(1, C, PLANES, ROWS * 128),
    )


def solution(mesh):
    in_specs = (
        P("tm", None, "space", None),
        P(None, "space", None),
        P(None, "space", None),
        P(),
        P(),
        P(),
        P(),
    )
    out_specs = (P("tm", None, "space", None), P("tm", None, "space", None))
    return jax.shard_map(shards, mesh=mesh, in_specs=in_specs, out_specs=out_specs, check_vma=False)
```
